128 devices in a mesh: tm: 4 (over z_hi, core), tile: 32 (over x, y, z_lo).
Axes of the slice: x: 4, y: 4, z: 4 (z_hi: 2, z_lo: 2; z = z_hi * 2 + z_lo), core: 2. Of those that a mesh axis runs over, the one named last changes fastest.
Arguments:
- features: bfloat16 [16, 32, 49152], P('tm', 'tile'), may hold values from -28 to 28
- first_gain: float32 [192], replicated, may hold values from 0.1 to 1.9
- first_kernel: bfloat16 [3, 3, 3, 192, 192], replicated, may hold values from -0.078125 to 0.078125
- first_offset: float32 [192], replicated, may hold values from -3 to 3
- second_gain: float32 [192], replicated, may hold values from 0.1 to 1.9
- second_kernel: bfloat16 [3, 3, 3, 192, 192], replicated, may hold values from -0.078125 to 0.078125
- second_offset: float32 [192], replicated, may hold values from -3 to 3
- upsample_kernel: bfloat16 [3, 3, 192, 96], replicated, may hold values from -0.15625 to 0.15625
- upsample_offset: float32 [96], replicated, may hold values from -3 to 3
Outputs:
- decoded: bfloat16 [16, 64, 49152], P('tm', 'tile')
The draws below stay inside these ranges and needn't reach their ends.
All inputs are finite; a program needn't handle non-finite values.
Results may differ from the reference program's by a relative error of at most 0.0052.
Values may be sent and summed in bfloat16 or wider, within the bound.
A program may use at most 128 MiB of HBM per device.

```python
import jax
import jax.numpy as jnp
from jax import lax

C = 192
C2 = 96
COLS = 256
FR = 16
ROWS = 32


def draw_features(key, part):
    key = jax.random.fold_in(key, 11)
    base_key, column_key, channel_key = jax.random.split(key, 3)
    row_place = jnp.arange(ROWS, dtype=jnp.float32) / max(ROWS - 1, 1)
    column_scale = jnp.exp(jax.random.uniform(column_key, (COLS, 1), minval=-0.69, maxval=0.69))
    channel_scale = jnp.exp(jax.random.uniform(channel_key, (1, C), minval=-0.69, maxval=0.69))
    base = jnp.clip(jax.random.normal(base_key, (FR, ROWS, COLS, C)), -4.0, 4.0)
    row_scale = 3.0 ** (row_place - 0.5)
    values = base * row_scale[None, :, None, None] * (column_scale * channel_scale)[None, None]
    return values.reshape(FR, ROWS, COLS * C).astype(jnp.bfloat16)


def centred(key, extent, spread, reach, kind=jnp.bfloat16):
    return jnp.clip(spread * jax.random.normal(key, extent, jnp.float32), -reach, reach).astype(kind)


def setup_inputs(seed: int = 0) -> dict:
    keys = jax.random.split(jax.random.key(seed), 10)
    return {
        "features": draw_features(jax.random.fold_in(keys[9], 71), 0),
        "first_gain": jnp.clip(1.0 + 0.18 * jax.random.normal(keys[1], (C,), jnp.float32), 0.1, 1.9),
        "first_kernel": centred(keys[2], (3, 3, 3, C, C), (27 * C) ** -0.5, 0.078125),
        "first_offset": centred(keys[3], (C,), 0.5, 3.0, jnp.float32),
        "second_gain": jnp.clip(1.0 + 0.18 * jax.random.normal(keys[4], (C,), jnp.float32), 0.1, 1.9),
        "second_kernel": centred(keys[5], (3, 3, 3, C, C), (27 * C) ** -0.5, 0.078125),
        "second_offset": centred(keys[6], (C,), 0.5, 3.0, jnp.float32),
        "upsample_kernel": centred(keys[7], (3, 3, C, C2), (9 * C) ** -0.5, 0.15625),
        "upsample_offset": centred(keys[8], (C2,), 0.5, 3.0, jnp.float32),
    }


epsilon = 1e-06

def norm_silu(hidden, gain):
    values = hidden.astype(jnp.float32)
    power = lax.optimization_barrier(jnp.mean(values * values, axis=3, keepdims=True))
    scaled = values * lax.rsqrt(power + epsilon) * gain
    return jax.nn.silu(scaled).astype(jnp.bfloat16)

def causal_conv(active, kernel, offset):
    padded = jnp.pad(active.astype(jnp.float32), ((2, 0), (1, 1), (1, 1), (0, 0)))
    result = lax.conv_general_dilated(padded[None], kernel.astype(jnp.float32), (1, 1, 1), 'VALID', dimension_numbers=('NDHWC', 'DHWIO', 'NDHWC'), precision=lax.Precision.HIGHEST)
    return result[0] + offset

def reference(features, first_gain, first_kernel, first_offset, second_gain, second_kernel, second_offset, upsample_kernel, upsample_offset):
    inputs = features.reshape(FR, ROWS, COLS, C)
    first_act = norm_silu(inputs, first_gain)
    hidden_one = causal_conv(first_act, first_kernel, first_offset)
    second_act = norm_silu(hidden_one, second_gain)
    hidden_two = causal_conv(second_act, second_kernel, second_offset)
    merged = (inputs.astype(jnp.float32) + hidden_two).astype(jnp.bfloat16)

    def upsample_picture(picture):
        doubled = jnp.repeat(jnp.repeat(picture, 2, axis=0), 2, axis=1).astype(jnp.float32)
        padded = jnp.pad(doubled, ((1, 1), (1, 1), (0, 0)))
        result = lax.conv_general_dilated(padded[None], upsample_kernel.astype(jnp.float32), (1, 1), 'VALID', dimension_numbers=('NHWC', 'HWIO', 'NHWC'), precision=lax.Precision.HIGHEST)[0]
        return (result + upsample_offset).astype(jnp.bfloat16).reshape(2 * ROWS, 2 * COLS * C2)
    return lax.map(upsample_picture, merged)
```

```python
import functools

import jax
import jax.numpy as jnp
from jax import lax
from jax.experimental import pallas as pl
from jax.experimental.pallas import tpu as pltpu
from jax.sharding import PartitionSpec as P

MESH = pl.DeviceIdType.MESH
EPS = 1e-06
F32 = jnp.float32
BF16 = jnp.bfloat16
PAIRS = 48
ACT1 = (6, 28, 42)
CONV1 = (7, 26, 41)
CONV2 = (7, 25, 41)
UPS = (8, 24, 40)
N = len(UPS) - 1
WINDOW = 40
SRC_PAIR = (0, 28, 60, 88)
DST_PAIR = (8, 4, 4, 0)


def pair_norm_silu(x0, x1, x2, gain, inside):
    low = lax.broadcasted_iota(jnp.int32, x1.shape, 1) < 64
    s1 = x1 * x1
    even = jnp.sum(x0 * x0 + jnp.where(low, s1, 0.0), axis=1, keepdims=True)
    odd = jnp.sum(x2 * x2 + jnp.where(low, 0.0, s1), axis=1, keepdims=True)
    even = lax.rsqrt(even * (1.0 / 192.0) + EPS)
    odd = lax.rsqrt(odd * (1.0 / 192.0) + EPS)
    scales = (even, jnp.where(low, even, odd), odd)
    outs = []
    for i, (x, s) in enumerate(zip((x0, x1, x2), scales)):
        v = x * s * gain[:, 128 * i : 128 * (i + 1)]
        v = v / (1.0 + jnp.exp(-v))
        outs.append(jnp.where(inside, v, 0.0).astype(BF16))
    return outs


def kernel(
    x_ref, w1_ref, w2_ref, uk_ref, vec_ref, out_ref,
    inb, xin, p1, p2, p3, we1, wo1, we2, wo2, ue, uo, fbuf, stage,
    in_send, in_recv, row_send, row_recv, out_send, out_recv, w_sem,
):
    tm = lax.axis_index("tm")
    tile = lax.axis_index("tile")
    zh, core = tm // 2, tm % 2
    big, zl = tile // 2, tile % 2
    z = zh * 2 + zl
    row = big * 2 + core
    has_up = row > 0
    has_down = row < 31

    def holder(r):
        return (zh * 2 + r % 2, (r // 2) * 2 + zl)

    barrier = pltpu.get_barrier_semaphore()
    for zz in range(4):
        for cc in range(2):
            partner = ((zl == cc) | (core == zz % 2)) & ~((z == zz) & (core == cc))

            @pl.when(partner)
            def _():
                pl.semaphore_signal(
                    barrier, inc=1, device_id=((zz // 2) * 2 + cc, big * 2 + zz % 2), device_id_type=MESH
                )

    outer = jnp.where(core == 1, row + 1, row - 1)
    has_outer = (outer >= 0) & (outer < 32)

    @pl.when(has_outer)
    def _():
        pl.semaphore_signal(barrier, inc=1, device_id=holder(outer), device_id_type=MESH)

    loads = [
        pltpu.make_async_copy(w1_ref, wo1.at[:, :, pl.ds(0, 576)], w_sem.at[0]),
        pltpu.make_async_copy(w1_ref.at[:, :, pl.ds(192, 384)], we1.at[:, :, pl.ds(0, 384)], w_sem.at[1]),
        pltpu.make_async_copy(w1_ref.at[:, :, pl.ds(0, 192)], we1.at[:, :, pl.ds(448, 192)], w_sem.at[2]),
        pltpu.make_async_copy(w2_ref, wo2.at[:, :, pl.ds(0, 576)], w_sem.at[3]),
        pltpu.make_async_copy(w2_ref.at[:, :, pl.ds(192, 384)], we2.at[:, :, pl.ds(0, 384)], w_sem.at[4]),
        pltpu.make_async_copy(w2_ref.at[:, :, pl.ds(0, 192)], we2.at[:, :, pl.ds(448, 192)], w_sem.at[5]),
    ]
    for load in loads:
        load.start()

    pl.semaphore_wait(barrier, jnp.where(zl == core, 5, 6) + has_outer.astype(jnp.int32))

    def reshard(zz):
        src = x_ref.at[pl.ds(12 * SRC_PAIR[zz], 12 * WINDOW)]
        dst = inb.at[tm, pl.ds(12 * DST_PAIR[zz], 12 * WINDOW)]
        local = pltpu.make_async_copy(src, dst, in_recv.at[tm])
        remote = pltpu.make_async_remote_copy(
            src_ref=src, dst_ref=dst, send_sem=in_send.at[zz], recv_sem=in_recv.at[tm],
            device_id=((zz // 2) * 2 + zl, big * 2 + zz % 2), device_id_type=MESH,
        )
        return (z == zz) & (zl == core), local, remote

    for zz in range(4):
        mine, local, remote = reshard(zz)
        pl.when(mine)(local.start)
        pl.when(~mine)(remote.start)

    zeros64 = jnp.zeros((3, 3, 64, 192), BF16)
    we1[:, :, 384:448] = zeros64
    wo1[:, :, 576:640] = zeros64
    we2[:, :, 384:448] = zeros64
    wo2[:, :, 576:640] = zeros64
    for buf in (p2, p3):
        for b in (6, 41):
            buf[:, 16 * b : 16 * b + 16] = jnp.zeros((3, 16, 384), BF16)

    @pl.when(~has_up)
    def _():
        for buf in (p1, p2, p3):
            buf[0] = jnp.zeros((16 * PAIRS, 384), BF16)

    @pl.when(~has_down)
    def _():
        for buf in (p1, p2, p3):
            buf[2] = jnp.zeros((16 * PAIRS, 384), BF16)

    src_lane = lax.broadcasted_iota(jnp.int32, (96, 256), 0)
    dst_lane = lax.broadcasted_iota(jnp.int32, (96, 256), 1)
    for u_ref, shift in ((ue, 0), (uo, 64)):
        sel_a = jnp.where(dst_lane == src_lane + shift, 1.0, 0.0).astype(BF16)
        sel_b = jnp.where(dst_lane == src_lane + shift + 96, 1.0, 0.0).astype(BF16)
        parts = []
        for q in range(3):
            a = [jnp.dot(uk_ref[q, s], sel_a, preferred_element_type=F32) for s in range(3)]
            b = [jnp.dot(uk_ref[q, s], sel_b, preferred_element_type=F32) for s in range(3)]
            parts.append((a[0], a[1] + a[2] + b[0] + b[1], b[2]))
        for phase, tap, rows in ((0, 0, (0,)), (0, 1, (1, 2)), (1, 0, (0, 1)), (1, 1, (2,))):
            left, mid, right = [
                functools.reduce(lambda m, n: m + n, [parts[q][i] for q in rows]).astype(BF16) for i in range(3)
            ]
            base = 640 * tap
            blank = jnp.zeros((64, 256), BF16)
            order = (mid, right, blank, left) if shift == 0 else (left, mid, right, blank)
            for block in order:
                u_ref[phase, base : base + block.shape[0]] = block
                base += block.shape[0]

    def inside_mask(first, rows):
        pair = lax.broadcasted_iota(jnp.int32, (rows, 128), 0) // 16 + first + (32 * z - 8)
        return (pair >= 0) & (pair < 128)

    def row_copies(st, buf, chunk, lo, hi):
        rows = pl.ds(16 * lo, 16 * (hi - lo))
        copies = []
        for d, (to, slot, exists) in enumerate(((row + 1, 0, has_down), (row - 1, 2, has_up))):
            copies.append((exists, pltpu.make_async_remote_copy(
                src_ref=buf.at[1, rows], dst_ref=buf.at[slot, rows],
                send_sem=row_send.at[st, d, chunk], recv_sem=row_recv.at[st, d, chunk],
                device_id=holder(to), device_id_type=MESH,
            )))
        return copies

    def send_rows(st, buf, chunk, lo, hi):
        for exists, copy in row_copies(st, buf, chunk, lo, hi):
            pl.when(exists)(copy.start)

    def wait_sent(st, buf, chunk, lo, hi):
        for exists, copy in row_copies(st, buf, chunk, lo, hi):
            pl.when(exists)(copy.wait_send)

    def wait_rows(st, buf, chunk, lo, hi):
        rows = pl.ds(16 * lo, 16 * (hi - lo))
        for d, (slot, exists) in enumerate(((0, has_up), (2, has_down))):
            ref = buf.at[slot, rows]
            pl.when(exists)(pltpu.make_async_copy(ref, ref, row_recv.at[st, d, chunk]).wait)

    gain1 = vec_ref[0:1, :]
    off1 = vec_ref[1:2, :]
    gain2 = vec_ref[2:3, :]
    off2 = vec_ref[3:4, :]
    off3 = vec_ref[4:5, :]

    for g in range(4):
        ref = inb.at[g, pl.ds(0, 12 * WINDOW)]
        pltpu.make_async_copy(ref, ref, in_recv.at[g]).wait()

    def act1(i):
        first = 4 + 4 * i
        start = pl.multiple_of(48 * i + 48, 16)
        groups = [inb[g, pl.ds(start, 48), :].astype(F32) for g in range(4)]
        tiles = [
            jnp.concatenate([g[4 * k : 4 * k + 4] for g in groups], axis=0) for k in range(12)
        ]
        x = [jnp.concatenate(tiles[i3::3], axis=0) for i3 in range(3)]
        acts = pair_norm_silu(*x, gain1, inside_mask(first, 64))
        rows = pl.ds(pl.multiple_of(64 * i + 64, 64), 64)
        for n in range(3):
            xin[rows, 128 * n : 128 * (n + 1)] = x[n].astype(BF16)
            p1[1, rows, 128 * n : 128 * (n + 1)] = acts[n]

    done = 4
    for chunk in range(N):
        end = -(-ACT1[chunk + 1] // 4) * 4
        lax.fori_loop((done - 4) // 4, (end - 4) // 4, lambda i, c: (act1(i), c)[1], 0)
        done = end
        send_rows(0, p1, chunk, ACT1[chunk], ACT1[chunk + 1])

    def conv(buf, we, wo, lo, hi):
        m = 16 * (hi - lo)
        here, before, after = (pl.ds(16 * (lo + k), m) for k in (0, -1, 1))
        even, odd = [], []
        for q in range(3):
            even += [buf[q, here, :], buf[q, before, 128:384]]
            odd += [buf[q, here, :], buf[q, after, 0:256]]
        outs = []
        t = lax.broadcasted_iota(jnp.int32, (m, 192), 0) % 16
        for lhs, w in ((even, we), (odd, wo)):
            lhs = jnp.concatenate(lhs, axis=1)
            y = [jnp.dot(lhs, w[p].reshape(1920, 192), preferred_element_type=F32) for p in range(3)]
            total = y[2] + jnp.where(t >= 1, pltpu.roll(y[1], 1, 0), 0.0)
            total = total + jnp.where(t >= 2, pltpu.roll(y[0], 2, 0), 0.0)
            outs.append(total)
        e, o = outs
        blank = jnp.zeros((m, 64), F32)
        o = pltpu.roll(jnp.concatenate([o, blank], axis=1), 64, 1)
        e = jnp.concatenate([e, blank], axis=1)
        return [e[:, :128], e[:, 128:] + o[:, :128], o[:, 128:]]

    def conv1(chunk):
        lo, hi = CONV1[chunk], CONV1[chunk + 1]
        x = conv(p1, we1, wo1, lo, hi)
        x = [v + off1[:, 128 * n : 128 * (n + 1)] for n, v in enumerate(x)]
        acts = pair_norm_silu(*x, gain2, inside_mask(lo, 16 * (hi - lo)))
        for n in range(3):
            p2[1, 16 * lo : 16 * hi, 128 * n : 128 * (n + 1)] = acts[n]

    def conv2(chunk):
        lo, hi = CONV2[chunk], CONV2[chunk + 1]
        x = conv(p2, we2, wo2, lo, hi)
        inside = inside_mask(lo, 16 * (hi - lo))
        for n in range(3):
            lanes = slice(128 * n, 128 * (n + 1))
            v = xin[16 * lo : 16 * hi, lanes].astype(F32) + (x[n] + off2[:, lanes])
            p3[1, 16 * lo : 16 * hi, lanes] = jnp.where(inside, v, 0.0).astype(BF16)

    def upsample(chunk):
        lo, hi = UPS[chunk], UPS[chunk + 1]
        n = hi - lo
        m = 16 * n
        here, before, after = (pl.ds(16 * (lo + k), m) for k in (0, -1, 1))
        for a in range(2):
            even, odd = [], []
            for q in (a, a + 1):
                even += [p3[q, here, :], p3[q, before, 128:384]]
                odd += [p3[q, here, :], p3[q, after, 0:256]]
            e = jnp.dot(jnp.concatenate(even, axis=1), ue[a], preferred_element_type=F32)
            o = jnp.dot(jnp.concatenate(odd, axis=1), uo[a], preferred_element_type=F32)
            tiles = [e[:, :128], e[:, 128:] + o[:, :128], o[:, 128:]]
            for i3 in range(3):
                v = tiles[i3] + off3[:, 128 * i3 : 128 * (i3 + 1)]
                for j in range(n):
                    fbuf[pl.ds(16 * (6 * j + 2 * i3 + a), 16), :] = v[16 * j : 16 * j + 16]
        for t in range(16):
            v = fbuf[pl.ds(t, 6 * n, stride=16), :]
            stage[t, 6 * (lo - 8) : 6 * (hi - 8), :] = v.astype(BF16)

    def out_copies(chunk):
        lo, hi = 6 * (UPS[chunk] - 8), 6 * (UPS[chunk + 1] - 8)
        copies = []
        for g in range(4):
            src = stage.at[pl.ds(4 * g, 4), pl.ds(lo, hi - lo)]
            dst = out_ref.at[:, pl.ds(pl.multiple_of(192 * z + lo, 16), hi - lo)]
            local = pltpu.make_async_copy(src, dst, out_recv.at[chunk, z])
            remote = pltpu.make_async_remote_copy(
                src_ref=src, dst_ref=dst, send_sem=out_send.at[chunk, g], recv_sem=out_recv.at[chunk, z],
                device_id=(g, big * 2 + core), device_id_type=MESH,
            )
            copies.append(((tm == g) & (zl == core), local, remote))
        return copies

    for load in loads[:3]:
        load.wait()
    for chunk in range(N):
        wait_rows(0, p1, chunk, ACT1[chunk], ACT1[chunk + 1])
        conv1(chunk)
        send_rows(1, p2, chunk, CONV1[chunk], CONV1[chunk + 1])
    for load in loads[3:]:
        load.wait()
    for chunk in range(N):
        wait_rows(1, p2, chunk, CONV1[chunk], CONV1[chunk + 1])
        conv2(chunk)
        send_rows(2, p3, chunk, CONV2[chunk], CONV2[chunk + 1])
    for chunk in range(N):
        wait_rows(2, p3, chunk, CONV2[chunk], CONV2[chunk + 1])
        upsample(chunk)
        for mine, local, remote in out_copies(chunk):
            pl.when(mine)(local.start)
            pl.when(~mine)(remote.start)

    for zz in range(4):
        mine, local, remote = reshard(zz)
        pl.when(~mine)(remote.wait_send)
    for chunk in range(N):
        wait_sent(0, p1, chunk, ACT1[chunk], ACT1[chunk + 1])
        wait_sent(1, p2, chunk, CONV1[chunk], CONV1[chunk + 1])
        wait_sent(2, p3, chunk, CONV2[chunk], CONV2[chunk + 1])
    for chunk in range(N):
        for mine, local, remote in out_copies(chunk):
            pl.when(~mine)(remote.wait_send)
        for zz in range(4):
            lo, hi = 6 * (UPS[chunk] - 8), 6 * (UPS[chunk + 1] - 8)
            ref = out_ref.at[:, pl.ds(192 * zz + lo, hi - lo)]
            pltpu.make_async_copy(ref, ref, out_recv.at[chunk, zz]).wait()


def shards(features, gain1, kernel1, offset1, gain2, kernel2, offset2, up_kernel, up_offset):
    x = features.reshape(4, 384, 128).transpose(1, 0, 2).reshape(1536, 128)
    vec = jnp.stack(
        [jnp.tile(v, 2) for v in (gain1, offset1, gain2, offset2)] + [jnp.tile(up_offset, 4)] + [jnp.zeros(384)] * 3
    )
    dma = pltpu.SemaphoreType.DMA
    act = pltpu.VMEM((3, 16 * PAIRS, 384), BF16)
    weights = pltpu.VMEM((3, 3, 640, 192), BF16)
    out = pl.pallas_call(
        kernel,
        out_shape=jax.ShapeDtypeStruct((4, 768, 128), BF16),
        in_specs=[pl.BlockSpec(memory_space=pl.ANY)] * 3 + [pl.BlockSpec(memory_space=pltpu.VMEM)] * 2,
        out_specs=pl.BlockSpec(memory_space=pl.ANY),
        scratch_shapes=[
            pltpu.VMEM((4, 12 * PAIRS, 128), BF16),
            pltpu.VMEM((16 * PAIRS, 384), BF16),
            act, act, act,
            weights, weights, weights, weights,
            pltpu.VMEM((2, 1280, 256), BF16),
            pltpu.VMEM((2, 1280, 256), BF16),
            pltpu.VMEM((16 * 96, 128), F32),
            pltpu.VMEM((16, 192, 128), BF16),
            dma((4,)), dma((4,)),
            dma((3, 2, N)), dma((3, 2, N)),
            dma((N, 4)), dma((N, 4)),
            dma((6,)),
        ],
        compiler_params=pltpu.CompilerParams(
            collective_id=0, has_side_effects=True, vmem_limit_bytes=48 * 1024 * 1024
        ),
    )(x, kernel1.reshape(3, 3, 576, 192), kernel2.reshape(3, 3, 576, 192), up_kernel, vec)
    return out.reshape(4, 384, 2, 128).transpose(0, 2, 1, 3).reshape(4, 2, 49152)


def solution(mesh):
    placed = (P("tm", "tile", None), P(), P(), P(), P(), P(), P(), P(), P())
    return jax.shard_map(
        shards, mesh=mesh, in_specs=placed, out_specs=P("tm", "tile", None), check_vma=False
    )
```

```python
import functools

import jax
import jax.numpy as jnp
from jax import lax
from jax.experimental import pallas as pl
from jax.experimental.pallas import tpu as pltpu
from jax.sharding import PartitionSpec as P

MESH = pl.DeviceIdType.MESH
EPS = 1e-06
F32 = jnp.float32
BF16 = jnp.bfloat16
PAIRS = 48
ACT1 = (6, 28, 42)
CONV1 = (7, 26, 41)
CONV2 = (7, 25, 41)
UPS = (8, 24, 40)
N = len(UPS) - 1
WINDOW = 40
SRC_PAIR = (0, 28, 60, 88)
DST_PAIR = (8, 4, 4, 0)


def pair_norm_silu(x0, x1, x2, gain, inside):
    low = lax.broadcasted_iota(jnp.int32, x1.shape, 1) < 64
    s1 = x1 * x1
    even = jnp.sum(x0 * x0 + jnp.where(low, s1, 0.0), axis=1, keepdims=True)
    odd = jnp.sum(x2 * x2 + jnp.where(low, 0.0, s1), axis=1, keepdims=True)
    even = lax.rsqrt(even * (1.0 / 192.0) + EPS)
    odd = lax.rsqrt(odd * (1.0 / 192.0) + EPS)
    scales = (even, jnp.where(low, even, odd), odd)
    outs = []
    for i, (x, s) in enumerate(zip((x0, x1, x2), scales)):
        v = x * s * gain[:, 128 * i : 128 * (i + 1)]
        v = v / (1.0 + jnp.exp(-v))
        outs.append(jnp.where(inside, v, 0.0).astype(BF16))
    return outs


def kernel(
    x_ref, w1_ref, w2_ref, up_ref, g1_ref, o1_ref, g2_ref, o2_ref, o3_ref, out_ref,
    inb, xin, p1, p2, p3, we1, wo1, we2, wo2, ue, uo, fbuf, stage, uk_ref, vg1, vo1, vg2, vo2, vo3,
    in_send, in_recv, row_send, row_recv, out_send, out_recv, w_sem,
):
    tm = lax.axis_index("tm")
    tile = lax.axis_index("tile")
    zh, core = tm // 2, tm % 2
    big, zl = tile // 2, tile % 2
    z = zh * 2 + zl
    row = big * 2 + core
    has_up = row > 0
    has_down = row < 31

    def holder(r):
        return (zh * 2 + r % 2, (r // 2) * 2 + zl)

    barrier = pltpu.get_barrier_semaphore()
    for zz in range(4):
        for cc in range(2):
            partner = ((zl == cc) | (core == zz % 2)) & ~((z == zz) & (core == cc))

            @pl.when(partner)
            def _():
                pl.semaphore_signal(
                    barrier, inc=1, device_id=((zz // 2) * 2 + cc, big * 2 + zz % 2), device_id_type=MESH
                )

    outer = jnp.where(core == 1, row + 1, row - 1)
    has_outer = (outer >= 0) & (outer < 32)

    @pl.when(has_outer)
    def _():
        pl.semaphore_signal(barrier, inc=1, device_id=holder(outer), device_id_type=MESH)

    loads = [
        pltpu.make_async_copy(w1_ref, wo1.at[:, :, pl.ds(0, 576)], w_sem.at[0]),
        pltpu.make_async_copy(w1_ref.at[:, :, pl.ds(192, 384)], we1.at[:, :, pl.ds(0, 384)], w_sem.at[1]),
        pltpu.make_async_copy(w1_ref.at[:, :, pl.ds(0, 192)], we1.at[:, :, pl.ds(448, 192)], w_sem.at[2]),
        pltpu.make_async_copy(w2_ref, wo2.at[:, :, pl.ds(0, 576)], w_sem.at[3]),
        pltpu.make_async_copy(w2_ref.at[:, :, pl.ds(192, 384)], we2.at[:, :, pl.ds(0, 384)], w_sem.at[4]),
        pltpu.make_async_copy(w2_ref.at[:, :, pl.ds(0, 192)], we2.at[:, :, pl.ds(448, 192)], w_sem.at[5]),
    ]
    small = [
        pltpu.make_async_copy(ref, to, w_sem.at[6 + i])
        for i, (ref, to) in enumerate(
            ((g1_ref, vg1), (o1_ref, vo1), (g2_ref, vg2), (o2_ref, vo2), (o3_ref, vo3))
        )
    ] + [pltpu.make_async_copy(up_ref, uk_ref, w_sem.at[11])]
    for load in small + loads:
        load.start()

    pl.semaphore_wait(barrier, jnp.where(zl == core, 5, 6) + has_outer.astype(jnp.int32))

    def reshard(zz):
        src = x_ref.at[pl.ds(12 * SRC_PAIR[zz], 12 * WINDOW)]
        dst = inb.at[tm, pl.ds(12 * DST_PAIR[zz], 12 * WINDOW)]
        local = pltpu.make_async_copy(src, dst, in_recv.at[tm])
        remote = pltpu.make_async_remote_copy(
            src_ref=src, dst_ref=dst, send_sem=in_send.at[zz], recv_sem=in_recv.at[tm],
            device_id=((zz // 2) * 2 + zl, big * 2 + zz % 2), device_id_type=MESH,
        )
        return (z == zz) & (zl == core), local, remote

    for zz in range(4):
        mine, local, remote = reshard(zz)
        pl.when(mine)(local.start)
        pl.when(~mine)(remote.start)

    zeros64 = jnp.zeros((3, 3, 64, 192), BF16)
    we1[:, :, 384:448] = zeros64
    wo1[:, :, 576:640] = zeros64
    we2[:, :, 384:448] = zeros64
    wo2[:, :, 576:640] = zeros64
    for buf in (p2, p3):
        for b in (6, 41):
            buf[:, 16 * b : 16 * b + 16] = jnp.zeros((3, 16, 384), BF16)

    @pl.when(~has_up)
    def _():
        for buf in (p1, p2, p3):
            buf[0] = jnp.zeros((16 * PAIRS, 384), BF16)

    @pl.when(~has_down)
    def _():
        for buf in (p1, p2, p3):
            buf[2] = jnp.zeros((16 * PAIRS, 384), BF16)

    for load in small:
        load.wait()
    src_lane = lax.broadcasted_iota(jnp.int32, (96, 256), 0)
    dst_lane = lax.broadcasted_iota(jnp.int32, (96, 256), 1)
    for u_ref, shift in ((ue, 0), (uo, 64)):
        sel_a = jnp.where(dst_lane == src_lane + shift, 1.0, 0.0).astype(BF16)
        sel_b = jnp.where(dst_lane == src_lane + shift + 96, 1.0, 0.0).astype(BF16)
        parts = []
        for q in range(3):
            a = [jnp.dot(uk_ref[q, s], sel_a, preferred_element_type=F32) for s in range(3)]
            b = [jnp.dot(uk_ref[q, s], sel_b, preferred_element_type=F32) for s in range(3)]
            parts.append((a[0], a[1] + a[2] + b[0] + b[1], b[2]))
        for phase, tap, rows in ((0, 0, (0,)), (0, 1, (1, 2)), (1, 0, (0, 1)), (1, 1, (2,))):
            left, mid, right = [
                functools.reduce(lambda m, n: m + n, [parts[q][i] for q in rows]).astype(BF16) for i in range(3)
            ]
            base = 640 * tap
            blank = jnp.zeros((64, 256), BF16)
            order = (mid, right, blank, left) if shift == 0 else (left, mid, right, blank)
            for block in order:
                u_ref[phase, base : base + block.shape[0]] = block
                base += block.shape[0]

    def inside_mask(first, rows):
        pair = lax.broadcasted_iota(jnp.int32, (rows, 128), 0) // 16 + first + (32 * z - 8)
        return (pair >= 0) & (pair < 128)

    def row_copies(st, buf, chunk, lo, hi):
        rows = pl.ds(16 * lo, 16 * (hi - lo))
        copies = []
        for d, (to, slot, exists) in enumerate(((row + 1, 0, has_down), (row - 1, 2, has_up))):
            copies.append((exists, pltpu.make_async_remote_copy(
                src_ref=buf.at[1, rows], dst_ref=buf.at[slot, rows],
                send_sem=row_send.at[st, d, chunk], recv_sem=row_recv.at[st, d, chunk],
                device_id=holder(to), device_id_type=MESH,
            )))
        return copies

    def send_rows(st, buf, chunk, lo, hi):
        for exists, copy in row_copies(st, buf, chunk, lo, hi):
            pl.when(exists)(copy.start)

    def wait_sent(st, buf, chunk, lo, hi):
        for exists, copy in row_copies(st, buf, chunk, lo, hi):
            pl.when(exists)(copy.wait_send)

    def wait_rows(st, buf, chunk, lo, hi):
        rows = pl.ds(16 * lo, 16 * (hi - lo))
        for d, (slot, exists) in enumerate(((0, has_up), (2, has_down))):
            ref = buf.at[slot, rows]
            pl.when(exists)(pltpu.make_async_copy(ref, ref, row_recv.at[st, d, chunk]).wait)

    lane8 = lax.broadcasted_iota(jnp.int32, (8, 128), 1)

    def widened(ref):
        v = jnp.concatenate([ref[...], jnp.zeros((1, 256 - ref.shape[1]), F32)], axis=1)
        return jnp.broadcast_to(v, (8, 256))

    def doubled(ref):
        v = widened(ref)
        r = pltpu.roll(v, 64, 1)
        return jnp.concatenate([v[:, :128], jnp.where(lane8 < 64, v[:, 128:], r[:, :128]), r[:, 128:]], axis=1)[0:1]

    gain1, off1, gain2, off2 = [doubled(ref) for ref in (vg1, vo1, vg2, vo2)]
    quarter = jnp.concatenate([widened(vo3), jnp.zeros((8, 128), F32)], axis=1)
    off3 = (quarter + pltpu.roll(quarter, 96, 1) + pltpu.roll(quarter, 192, 1) + pltpu.roll(quarter, 288, 1))[0:1]

    for g in range(4):
        ref = inb.at[g, pl.ds(0, 12 * WINDOW)]
        pltpu.make_async_copy(ref, ref, in_recv.at[g]).wait()

    def act1(i):
        first = 4 + 4 * i
        start = pl.multiple_of(48 * i + 48, 16)
        groups = [inb[g, pl.ds(start, 48), :].astype(F32) for g in range(4)]
        tiles = [
            jnp.concatenate([g[4 * k : 4 * k + 4] for g in groups], axis=0) for k in range(12)
        ]
        x = [jnp.concatenate(tiles[i3::3], axis=0) for i3 in range(3)]
        acts = pair_norm_silu(*x, gain1, inside_mask(first, 64))
        rows = pl.ds(pl.multiple_of(64 * i + 64, 64), 64)
        for n in range(3):
            xin[rows, 128 * n : 128 * (n + 1)] = x[n].astype(BF16)
            p1[1, rows, 128 * n : 128 * (n + 1)] = acts[n]

    done = 4
    for chunk in range(N):
        end = -(-ACT1[chunk + 1] // 4) * 4
        lax.fori_loop((done - 4) // 4, (end - 4) // 4, lambda i, c: (act1(i), c)[1], 0)
        done = end
        send_rows(0, p1, chunk, ACT1[chunk], ACT1[chunk + 1])

    def conv(buf, we, wo, lo, hi):
        m = 16 * (hi - lo)
        here, before, after = (pl.ds(16 * (lo + k), m) for k in (0, -1, 1))
        even, odd = [], []
        for q in range(3):
            even += [buf[q, here, :], buf[q, before, 128:384]]
            odd += [buf[q, here, :], buf[q, after, 0:256]]
        outs = []
        t = lax.broadcasted_iota(jnp.int32, (m, 192), 0) % 16
        for lhs, w in ((even, we), (odd, wo)):
            lhs = jnp.concatenate(lhs, axis=1)
            y = [jnp.dot(lhs, w[p].reshape(1920, 192), preferred_element_type=F32) for p in range(3)]
            total = y[2] + jnp.where(t >= 1, pltpu.roll(y[1], 1, 0), 0.0)
            total = total + jnp.where(t >= 2, pltpu.roll(y[0], 2, 0), 0.0)
            outs.append(total)
        e, o = outs
        blank = jnp.zeros((m, 64), F32)
        o = pltpu.roll(jnp.concatenate([o, blank], axis=1), 64, 1)
        e = jnp.concatenate([e, blank], axis=1)
        return [e[:, :128], e[:, 128:] + o[:, :128], o[:, 128:]]

    def conv1(chunk):
        lo, hi = CONV1[chunk], CONV1[chunk + 1]
        x = conv(p1, we1, wo1, lo, hi)
        x = [v + off1[:, 128 * n : 128 * (n + 1)] for n, v in enumerate(x)]
        acts = pair_norm_silu(*x, gain2, inside_mask(lo, 16 * (hi - lo)))
        for n in range(3):
            p2[1, 16 * lo : 16 * hi, 128 * n : 128 * (n + 1)] = acts[n]

    def conv2(chunk):
        lo, hi = CONV2[chunk], CONV2[chunk + 1]
        x = conv(p2, we2, wo2, lo, hi)
        inside = inside_mask(lo, 16 * (hi - lo))
        for n in range(3):
            lanes = slice(128 * n, 128 * (n + 1))
            v = xin[16 * lo : 16 * hi, lanes].astype(F32) + (x[n] + off2[:, lanes])
            p3[1, 16 * lo : 16 * hi, lanes] = jnp.where(inside, v, 0.0).astype(BF16)

    def upsample(chunk):
        lo, hi = UPS[chunk], UPS[chunk + 1]
        n = hi - lo
        m = 16 * n
        here, before, after = (pl.ds(16 * (lo + k), m) for k in (0, -1, 1))
        for a in range(2):
            even, odd = [], []
            for q in (a, a + 1):
                even += [p3[q, here, :], p3[q, before, 128:384]]
                odd += [p3[q, here, :], p3[q, after, 0:256]]
            e = jnp.dot(jnp.concatenate(even, axis=1), ue[a], preferred_element_type=F32)
            o = jnp.dot(jnp.concatenate(odd, axis=1), uo[a], preferred_element_type=F32)
            tiles = [e[:, :128], e[:, 128:] + o[:, :128], o[:, 128:]]
            for i3 in range(3):
                v = tiles[i3] + off3[:, 128 * i3 : 128 * (i3 + 1)]
                for j in range(n):
                    fbuf[pl.ds(16 * (6 * j + 2 * i3 + a), 16), :] = v[16 * j : 16 * j + 16]
        for t in range(16):
            v = fbuf[pl.ds(t, 6 * n, stride=16), :]
            stage[t, 6 * (lo - 8) : 6 * (hi - 8), :] = v.astype(BF16)

    def out_copies(chunk):
        lo, hi = 6 * (UPS[chunk] - 8), 6 * (UPS[chunk + 1] - 8)
        copies = []
        for g in range(4):
            src = stage.at[pl.ds(4 * g, 4), pl.ds(lo, hi - lo)]
            dst = out_ref.at[:, pl.ds(pl.multiple_of(192 * z + lo, 16), hi - lo)]
            local = pltpu.make_async_copy(src, dst, out_recv.at[chunk, z])
            remote = pltpu.make_async_remote_copy(
                src_ref=src, dst_ref=dst, send_sem=out_send.at[chunk, g], recv_sem=out_recv.at[chunk, z],
                device_id=(g, big * 2 + core), device_id_type=MESH,
            )
            copies.append(((tm == g) & (zl == core), local, remote))
        return copies

    for load in loads[:3]:
        load.wait()
    for chunk in range(N):
        wait_rows(0, p1, chunk, ACT1[chunk], ACT1[chunk + 1])
        conv1(chunk)
        send_rows(1, p2, chunk, CONV1[chunk], CONV1[chunk + 1])
    for load in loads[3:]:
        load.wait()
    for chunk in range(N):
        wait_rows(1, p2, chunk, CONV1[chunk], CONV1[chunk + 1])
        conv2(chunk)
        send_rows(2, p3, chunk, CONV2[chunk], CONV2[chunk + 1])
    for chunk in range(N):
        wait_rows(2, p3, chunk, CONV2[chunk], CONV2[chunk + 1])
        upsample(chunk)
        for mine, local, remote in out_copies(chunk):
            pl.when(mine)(local.start)
            pl.when(~mine)(remote.start)

    for zz in range(4):
        mine, local, remote = reshard(zz)
        pl.when(~mine)(remote.wait_send)
    for chunk in range(N):
        wait_sent(0, p1, chunk, ACT1[chunk], ACT1[chunk + 1])
        wait_sent(1, p2, chunk, CONV1[chunk], CONV1[chunk + 1])
        wait_sent(2, p3, chunk, CONV2[chunk], CONV2[chunk + 1])
    for chunk in range(N):
        for mine, local, remote in out_copies(chunk):
            pl.when(~mine)(remote.wait_send)
        for zz in range(4):
            lo, hi = 6 * (UPS[chunk] - 8), 6 * (UPS[chunk + 1] - 8)
            ref = out_ref.at[:, pl.ds(192 * zz + lo, hi - lo)]
            pltpu.make_async_copy(ref, ref, out_recv.at[chunk, zz]).wait()


def shards(features, gain1, kernel1, offset1, gain2, kernel2, offset2, up_kernel, up_offset):
    x = features.reshape(4, 384, 128).transpose(1, 0, 2).reshape(1536, 128)
    small = [v.reshape(1, -1) for v in (gain1, offset1, gain2, offset2, up_offset)]
    dma = pltpu.SemaphoreType.DMA
    act = pltpu.VMEM((3, 16 * PAIRS, 384), BF16)
    weights = pltpu.VMEM((3, 3, 640, 192), BF16)
    out = pl.pallas_call(
        kernel,
        out_shape=jax.ShapeDtypeStruct((4, 768, 128), BF16),
        in_specs=[pl.BlockSpec(memory_space=pl.ANY)] * 9,
        out_specs=pl.BlockSpec(memory_space=pl.ANY),
        scratch_shapes=[
            pltpu.VMEM((4, 12 * PAIRS, 128), BF16),
            pltpu.VMEM((16 * PAIRS, 384), BF16),
            act, act, act,
            weights, weights, weights, weights,
            pltpu.VMEM((2, 1280, 256), BF16),
            pltpu.VMEM((2, 1280, 256), BF16),
            pltpu.VMEM((16 * 96, 128), F32),
            pltpu.VMEM((16, 192, 128), BF16),
            pltpu.VMEM((3, 3, 192, 96), BF16),
            *[pltpu.VMEM((1, n), F32) for n in (192, 192, 192, 192, 96)],
            dma((4,)), dma((4,)),
            dma((3, 2, N)), dma((3, 2, N)),
            dma((N, 4)), dma((N, 4)),
            dma((12,)),
        ],
        compiler_params=pltpu.CompilerParams(
            collective_id=0, has_side_effects=True, vmem_limit_bytes=60 * 1024 * 1024
        ),
    )(x, kernel1.reshape(3, 3, 576, 192), kernel2.reshape(3, 3, 576, 192), up_kernel, *small)
    return out.reshape(4, 384, 2, 128).transpose(0, 2, 1, 3).reshape(4, 2, 49152)


def solution(mesh):
    placed = (P("tm", "tile", None), P(), P(), P(), P(), P(), P(), P(), P())
    return jax.shard_map(
        shards, mesh=mesh, in_specs=placed, out_specs=P("tm", "tile", None), check_vma=False
    )
```

```python
import functools

import jax
import jax.numpy as jnp
from jax import lax
from jax.experimental import pallas as pl
from jax.experimental.pallas import tpu as pltpu
from jax.sharding import PartitionSpec as P

MESH = pl.DeviceIdType.MESH
EPS = 1e-06
F32 = jnp.float32
BF16 = jnp.bfloat16
PAIRS = 48
INPUT = (4, 12, 20, 28, 36, 44)
ACT1 = (6, *INPUT[1:-1], 42)
CONV1 = (7, 11, 18, 26, 34, 41)
CONV2 = (7, 10, 17, 25, 33, 41)
UPS = (8, 16, 24, 32, 40)
BOUNDS = (ACT1, CONV1, CONV2, UPS)
COUNTS = tuple(len(b) - 1 for b in BOUNDS)
MOST = max(COUNTS)
ORDER = "00 01 02 03 10 04 11 12 13 20 14 21 22 23 24 30 31 32 33"


def pair_norm_silu(x0, x1, x2, gain, inside):
    low = lax.broadcasted_iota(jnp.int32, x1.shape, 1) < 64
    s1 = x1 * x1
    even = jnp.sum(x0 * x0 + jnp.where(low, s1, 0.0), axis=1, keepdims=True)
    odd = jnp.sum(x2 * x2 + jnp.where(low, 0.0, s1), axis=1, keepdims=True)
    even = lax.rsqrt(even * (1.0 / 192.0) + EPS)
    odd = lax.rsqrt(odd * (1.0 / 192.0) + EPS)
    scales = (even, jnp.where(low, even, odd), odd)
    outs = []
    for i, (x, s) in enumerate(zip((x0, x1, x2), scales)):
        v = x * s * gain[:, 128 * i : 128 * (i + 1)]
        v = v / (1.0 + jnp.exp(-v))
        outs.append(jnp.where(inside, v, 0.0).astype(BF16))
    return outs


def kernel(
    x_ref, w1_ref, w2_ref, up_ref, g1_ref, o1_ref, g2_ref, o2_ref, o3_ref, out_ref,
    inb, xin, p1, p2, p3, wb1, wb2, ue, uo, fbuf, stage, uk_ref, vg1, vo1, vg2, vo2, vo3,
    in_send, in_recv, row_send, row_recv, out_send, out_recv, w_sem,
):
    tm = lax.axis_index("tm")
    tile = lax.axis_index("tile")
    zh, core = tm // 2, tm % 2
    big, zl = tile // 2, tile % 2
    z = zh * 2 + zl
    row = big * 2 + core
    has_up = row > 0
    has_down = row < 31

    def holder(r):
        return (zh * 2 + r % 2, (r // 2) * 2 + zl)

    barrier = pltpu.get_barrier_semaphore()
    for zz in range(4):
        for cc in range(2):
            partner = ((zl == cc) | (core == zz % 2)) & ~((z == zz) & (core == cc))

            @pl.when(partner)
            def _():
                pl.semaphore_signal(
                    barrier, inc=1, device_id=((zz // 2) * 2 + cc, big * 2 + zz % 2), device_id_type=MESH
                )

    outer = jnp.where(core == 1, row + 1, row - 1)
    has_outer = (outer >= 0) & (outer < 32)

    @pl.when(has_outer)
    def _():
        pl.semaphore_signal(barrier, inc=1, device_id=holder(outer), device_id_type=MESH)

    loads = [
        pltpu.make_async_copy(ref, to.at[:, :, pl.ds(64, 576)], w_sem.at[i])
        for i, (ref, to) in enumerate(((w1_ref, wb1), (w2_ref, wb2)))
    ]
    small = [
        pltpu.make_async_copy(ref, to, w_sem.at[2 + i])
        for i, (ref, to) in enumerate(
            ((g1_ref, vg1), (o1_ref, vo1), (g2_ref, vg2), (o2_ref, vo2), (o3_ref, vo3))
        )
    ] + [pltpu.make_async_copy(up_ref, uk_ref, w_sem.at[7])]
    for load in small:
        load.start()

    for buf in (wb1, wb2):
        for base in (0, 640):
            buf[:, :, base : base + 64] = jnp.zeros((3, 3, 64, 192), BF16)
    for buf in (p2, p3):
        for b in (6, 41):
            buf[:, 16 * b : 16 * b + 16] = jnp.zeros((3, 16, 384), BF16)

    @pl.when(~has_up)
    def _():
        for buf in (p1, p2, p3):
            buf[0] = jnp.zeros((16 * PAIRS, 384), BF16)

    @pl.when(~has_down)
    def _():
        for buf in (p1, p2, p3):
            buf[2] = jnp.zeros((16 * PAIRS, 384), BF16)

    pl.semaphore_wait(barrier, jnp.where(zl == core, 5, 6) + has_outer.astype(jnp.int32))

    def windows(chunk):
        lo, hi = INPUT[chunk], INPUT[chunk + 1]
        if chunk == 0:
            return ((lambda zz: zz == 0, 8, hi), (lambda zz: zz != 0, lo, hi))
        if chunk == COUNTS[0] - 1:
            return ((lambda zz: zz == 3, lo, 40), (lambda zz: zz != 3, lo, hi))
        return ((lambda zz: zz >= 0, lo, hi),)

    def reshard(chunk, ahead, lo, hi):
        zz = (z + ahead) % 4
        src = x_ref.at[pl.ds(pl.multiple_of(12 * (lo - 8 + 32 * zz), 16), 12 * (hi - lo))]
        dst = inb.at[tm, pl.ds(12 * lo, 12 * (hi - lo))]
        local = pltpu.make_async_copy(src, dst, in_recv.at[chunk, tm])
        remote = pltpu.make_async_remote_copy(
            src_ref=src, dst_ref=dst, send_sem=in_send.at[chunk, ahead], recv_sem=in_recv.at[chunk, tm],
            device_id=((zz // 2) * 2 + zl, big * 2 + zz % 2), device_id_type=MESH,
        )
        return zz, local, remote

    for chunk in range(COUNTS[0]):
        for ahead in (2, 1, 3, 0):
            for fits, lo, hi in windows(chunk):
                zz, local, remote = reshard(chunk, ahead, lo, hi)
                if ahead == 0:
                    pl.when(fits(zz) & (zl == core))(local.start)
                    pl.when(fits(zz) & (zl != core))(remote.start)
                else:
                    pl.when(fits(zz))(remote.start)

    for load in loads:
        load.start()

    def wait_input(chunk):
        for fits, lo, hi in windows(chunk):

            @pl.when(fits(z))
            def _():
                for g in range(4):
                    ref = inb.at[g, pl.ds(12 * lo, 12 * (hi - lo))]
                    pltpu.make_async_copy(ref, ref, in_recv.at[chunk, g]).wait()

    def wait_input_sent(chunk):
        for ahead in range(4):
            for fits, lo, hi in windows(chunk):
                zz, local, remote = reshard(chunk, ahead, lo, hi)
                go = fits(zz) if ahead else fits(zz) & (zl != core)
                pl.when(go)(remote.wait_send)

    for load in small:
        load.wait()
    src_lane = lax.broadcasted_iota(jnp.int32, (96, 256), 0)
    dst_lane = lax.broadcasted_iota(jnp.int32, (96, 256), 1)
    for u_ref, shift in ((ue, 0), (uo, 64)):
        sel_a = jnp.where(dst_lane == src_lane + shift, 1.0, 0.0).astype(BF16)
        sel_b = jnp.where(dst_lane == src_lane + shift + 96, 1.0, 0.0).astype(BF16)
        parts = []
        for q in range(3):
            a = [jnp.dot(uk_ref[q, s], sel_a, preferred_element_type=F32) for s in range(3)]
            b = [jnp.dot(uk_ref[q, s], sel_b, preferred_element_type=F32) for s in range(3)]
            parts.append((a[0], a[1] + a[2] + b[0] + b[1], b[2]))
        for phase, tap, rows in ((0, 0, (0,)), (0, 1, (1, 2)), (1, 0, (0, 1)), (1, 1, (2,))):
            left, mid, right = [
                functools.reduce(lambda m, n: m + n, [parts[q][i] for q in rows]).astype(BF16) for i in range(3)
            ]
            base = 640 * tap
            blank = jnp.zeros((64, 256), BF16)
            order = (mid, right, blank, left) if shift == 0 else (left, mid, right, blank)
            for block in order:
                u_ref[phase, base : base + block.shape[0]] = block
                base += block.shape[0]

    def inside_mask(first, rows):
        pair = lax.broadcasted_iota(jnp.int32, (rows, 128), 0) // 16 + first + (32 * z - 8)
        return (pair >= 0) & (pair < 128)

    bufs = (p1, p2, p3)

    def chunk_rows(st, chunk):
        lo, hi = BOUNDS[st][chunk], BOUNDS[st][chunk + 1]
        return pl.ds(16 * lo, 16 * (hi - lo))

    def row_copies(st, chunk):
        buf, rows = bufs[st], chunk_rows(st, chunk)
        copies = []
        for d, (to, slot, exists) in enumerate(((row + 1, 0, has_down), (row - 1, 2, has_up))):
            copies.append((exists, pltpu.make_async_remote_copy(
                src_ref=buf.at[1, rows], dst_ref=buf.at[slot, rows],
                send_sem=row_send.at[st, d, chunk], recv_sem=row_recv.at[st, d, chunk],
                device_id=holder(to), device_id_type=MESH,
            )))
        return copies

    def send_rows(st, chunk):
        for exists, copy in row_copies(st, chunk):
            pl.when(exists)(copy.start)

    def wait_sent(st, chunk):
        for exists, copy in row_copies(st, chunk):
            pl.when(exists)(copy.wait_send)

    waited = [0, 0, 0]

    def wait_rows(st, end):
        while waited[st] < COUNTS[st] and BOUNDS[st][waited[st]] < end:
            chunk = waited[st]
            for d, (slot, exists) in enumerate(((0, has_up), (2, has_down))):
                ref = bufs[st].at[slot, chunk_rows(st, chunk)]
                pl.when(exists)(pltpu.make_async_copy(ref, ref, row_recv.at[st, d, chunk]).wait)
            waited[st] += 1

    lane8 = lax.broadcasted_iota(jnp.int32, (8, 128), 1)

    def widened(ref):
        v = jnp.concatenate([ref[...], jnp.zeros((1, 256 - ref.shape[1]), F32)], axis=1)
        return jnp.broadcast_to(v, (8, 256))

    def doubled(ref):
        v = widened(ref)
        r = pltpu.roll(v, 64, 1)
        return jnp.concatenate([v[:, :128], jnp.where(lane8 < 64, v[:, 128:], r[:, :128]), r[:, 128:]], axis=1)[0:1]

    gain1, off1, gain2, off2 = [doubled(ref) for ref in (vg1, vo1, vg2, vo2)]
    quarter = jnp.concatenate([widened(vo3), jnp.zeros((8, 128), F32)], axis=1)
    off3 = (quarter + pltpu.roll(quarter, 96, 1) + pltpu.roll(quarter, 192, 1) + pltpu.roll(quarter, 288, 1))[0:1]

    def act1_group(i):
        first = 4 + 4 * i
        start = 48 * i + 48
        groups = [inb[g, pl.ds(start, 48), :].astype(F32) for g in range(4)]
        tiles = [
            jnp.concatenate([g[4 * k : 4 * k + 4] for g in groups], axis=0) for k in range(12)
        ]
        x = [jnp.concatenate(tiles[i3::3], axis=0) for i3 in range(3)]
        acts = pair_norm_silu(*x, gain1, inside_mask(first, 64))
        rows = pl.ds(64 * i + 64, 64)
        for n in range(3):
            xin[rows, 128 * n : 128 * (n + 1)] = x[n].astype(BF16)
            p1[1, rows, 128 * n : 128 * (n + 1)] = acts[n]

    def act1(chunk):
        wait_input(chunk)
        for i in range(INPUT[chunk] // 4 - 1, INPUT[chunk + 1] // 4 - 1):
            act1_group(i)
        send_rows(0, chunk)

    def conv(buf, wb, lo, hi):
        m = 16 * (hi - lo)
        here, before, after = (pl.ds(16 * (lo + k), m) for k in (0, -1, 1))
        even, odd = [], []
        for q in range(3):
            even += [buf[q, before, 128:384], buf[q, here, :]]
            odd += [buf[q, here, :], buf[q, after, 0:256]]
        outs = []
        t = lax.broadcasted_iota(jnp.int32, (m, 192), 0) % 16
        for lhs, base in ((even, 0), (odd, 64)):
            lhs = jnp.concatenate(lhs, axis=1)
            y = [
                jnp.dot(lhs, wb[p, :, base : base + 640].reshape(1920, 192), preferred_element_type=F32)
                for p in range(3)
            ]
            total = y[2] + jnp.where(t >= 1, pltpu.roll(y[1], 1, 0), 0.0)
            total = total + jnp.where(t >= 2, pltpu.roll(y[0], 2, 0), 0.0)
            outs.append(total)
        e, o = outs
        blank = jnp.zeros((m, 64), F32)
        o = pltpu.roll(jnp.concatenate([o, blank], axis=1), 64, 1)
        e = jnp.concatenate([e, blank], axis=1)
        return [e[:, :128], e[:, 128:] + o[:, :128], o[:, 128:]]

    def conv1(chunk):
        if chunk == 0:
            loads[0].wait()
        lo, hi = CONV1[chunk], CONV1[chunk + 1]
        wait_rows(0, hi + 1)
        x = conv(p1, wb1, lo, hi)
        x = [v + off1[:, 128 * n : 128 * (n + 1)] for n, v in enumerate(x)]
        acts = pair_norm_silu(*x, gain2, inside_mask(lo, 16 * (hi - lo)))
        for n in range(3):
            p2[1, 16 * lo : 16 * hi, 128 * n : 128 * (n + 1)] = acts[n]
        send_rows(1, chunk)

    def conv2(chunk):
        if chunk == 0:
            loads[1].wait()
        lo, hi = CONV2[chunk], CONV2[chunk + 1]
        wait_rows(1, hi + 1)
        x = conv(p2, wb2, lo, hi)
        inside = inside_mask(lo, 16 * (hi - lo))
        for n in range(3):
            lanes = slice(128 * n, 128 * (n + 1))
            v = xin[16 * lo : 16 * hi, lanes].astype(F32) + (x[n] + off2[:, lanes])
            p3[1, 16 * lo : 16 * hi, lanes] = jnp.where(inside, v, 0.0).astype(BF16)
        send_rows(2, chunk)

    def upsample(chunk):
        lo, hi = UPS[chunk], UPS[chunk + 1]
        wait_rows(2, hi + 1)
        n = hi - lo
        m = 16 * n
        here, before, after = (pl.ds(16 * (lo + k), m) for k in (0, -1, 1))
        for a in range(2):
            even, odd = [], []
            for q in (a, a + 1):
                even += [p3[q, here, :], p3[q, before, 128:384]]
                odd += [p3[q, here, :], p3[q, after, 0:256]]
            e = jnp.dot(jnp.concatenate(even, axis=1), ue[a], preferred_element_type=F32)
            o = jnp.dot(jnp.concatenate(odd, axis=1), uo[a], preferred_element_type=F32)
            tiles = [e[:, :128], e[:, 128:] + o[:, :128], o[:, 128:]]
            for i3 in range(3):
                v = tiles[i3] + off3[:, 128 * i3 : 128 * (i3 + 1)]
                for j in range(n):
                    fbuf[pl.ds(16 * (6 * j + 2 * i3 + a), 16), :] = v[16 * j : 16 * j + 16]
        for t in range(16):
            v = fbuf[pl.ds(t, 6 * n, stride=16), :]
            stage[t, 6 * (lo - 8) : 6 * (hi - 8), :] = v.astype(BF16)

        for mine, local, remote in out_copies(chunk):
            pl.when(mine)(local.start)
            pl.when(~mine)(remote.start)

    def out_copies(chunk):
        lo, hi = 6 * (UPS[chunk] - 8), 6 * (UPS[chunk + 1] - 8)
        copies = []
        for g in range(4):
            src = stage.at[pl.ds(4 * g, 4), pl.ds(lo, hi - lo)]
            dst = out_ref.at[:, pl.ds(pl.multiple_of(192 * z + lo, 16), hi - lo)]
            local = pltpu.make_async_copy(src, dst, out_recv.at[chunk, z])
            remote = pltpu.make_async_remote_copy(
                src_ref=src, dst_ref=dst, send_sem=out_send.at[chunk, g], recv_sem=out_recv.at[chunk, z],
                device_id=(g, big * 2 + core), device_id_type=MESH,
            )
            copies.append(((tm == g) & (zl == core), local, remote))
        return copies

    for stage_chunk in ORDER.split():
        (act1, conv1, conv2, upsample)[int(stage_chunk[0])](int(stage_chunk[1]))

    for chunk in range(COUNTS[0]):
        wait_input_sent(chunk)
    for st in range(3):
        for chunk in range(COUNTS[st]):
            wait_sent(st, chunk)
    for chunk in range(COUNTS[3]):
        for mine, local, remote in out_copies(chunk):
            pl.when(~mine)(remote.wait_send)
        for zz in range(4):
            lo, hi = 6 * (UPS[chunk] - 8), 6 * (UPS[chunk + 1] - 8)
            ref = out_ref.at[:, pl.ds(192 * zz + lo, hi - lo)]
            pltpu.make_async_copy(ref, ref, out_recv.at[chunk, zz]).wait()


def shards(features, gain1, kernel1, offset1, gain2, kernel2, offset2, up_kernel, up_offset):
    x = features.reshape(4, 384, 128).transpose(1, 0, 2).reshape(1536, 128)
    small = [v.reshape(1, -1) for v in (gain1, offset1, gain2, offset2, up_offset)]
    dma = pltpu.SemaphoreType.DMA
    act = pltpu.VMEM((3, 16 * PAIRS, 384), BF16)
    weights = pltpu.VMEM((3, 3, 704, 192), BF16)
    out = pl.pallas_call(
        kernel,
        out_shape=pltpu.VMEM((4, 768, 128), BF16),
        in_specs=[pl.BlockSpec(memory_space=pl.ANY)] * 9,
        out_specs=pl.BlockSpec(memory_space=pl.ANY),
        scratch_shapes=[
            pltpu.VMEM((4, 12 * PAIRS, 128), BF16),
            pltpu.VMEM((16 * PAIRS, 384), BF16),
            act, act, act,
            weights, weights,
            pltpu.VMEM((2, 1280, 256), BF16),
            pltpu.VMEM((2, 1280, 256), BF16),
            pltpu.VMEM((16 * 96, 128), F32),
            pltpu.VMEM((16, 192, 128), BF16),
            pltpu.VMEM((3, 3, 192, 96), BF16),
            *[pltpu.VMEM((1, n), F32) for n in (192, 192, 192, 192, 96)],
            dma((COUNTS[0], 4)), dma((COUNTS[0], 4)),
            dma((3, 2, MOST)), dma((3, 2, MOST)),
            dma((COUNTS[3], 4)), dma((COUNTS[3], 4)),
            dma((8,)),
        ],
        compiler_params=pltpu.CompilerParams(
            collective_id=0, has_side_effects=True, vmem_limit_bytes=56 * 1024 * 1024
        ),
    )(x, kernel1.reshape(3, 3, 576, 192), kernel2.reshape(3, 3, 576, 192), up_kernel, *small)
    return out.reshape(4, 384, 2, 128).transpose(0, 2, 1, 3).reshape(4, 2, 49152)


def solution(mesh):
    placed = (P("tm", "tile", None), P(), P(), P(), P(), P(), P(), P(), P())
    return jax.shard_map(
        shards, mesh=mesh, in_specs=placed, out_specs=P("tm", "tile", None), check_vma=False
    )
```

```python
import functools

import jax
import jax.numpy as jnp
from jax import lax
from jax.experimental import pallas as pl
from jax.experimental.pallas import tpu as pltpu
from jax.sharding import PartitionSpec as P

MESH = pl.DeviceIdType.MESH
EPS = 1e-06
F32 = jnp.float32
BF16 = jnp.bfloat16
PAIRS = 48
INPUT = (4, 12, 20, 28, 36, 44)
ACT1 = (6, *INPUT[1:-1], 42)
CONV1 = (7, 18, 26, 34, 41)
CONV2 = (7, 17, 25, 33, 41)
UPS = (8, 16, 24, 32, 40)
BOUNDS = (ACT1, CONV1, CONV2, UPS)
COUNTS = tuple(len(b) - 1 for b in BOUNDS)
MOST = max(COUNTS)
OUT_ROWS = tuple(16 * (3 * (b - 8) // 16) for b in UPS)
ORDER = "00 01 02 03 04 10 11 12 13 20 21 30 22 31 23 32 40 41 42 33 43 50 51 52 53"


def pair_norm_silu(x0, x1, x2, gain, inside):
    low = lax.broadcasted_iota(jnp.int32, x1.shape, 1) < 64
    s1 = x1 * x1
    even = jnp.sum(x0 * x0 + jnp.where(low, s1, 0.0), axis=1, keepdims=True)
    odd = jnp.sum(x2 * x2 + jnp.where(low, 0.0, s1), axis=1, keepdims=True)
    even = lax.rsqrt(even * (1.0 / 192.0) + EPS)
    odd = lax.rsqrt(odd * (1.0 / 192.0) + EPS)
    scales = (even, jnp.where(low, even, odd), odd)
    outs = []
    for i, (x, s) in enumerate(zip((x0, x1, x2), scales)):
        v = x * s * gain[:, 128 * i : 128 * (i + 1)]
        v = v / (1.0 + jnp.exp(-v))
        outs.append(jnp.where(inside, v, 0.0).astype(BF16))
    return outs


def kernel(
    x_ref, w1_ref, w2_ref, up_ref, g1_ref, o1_ref, g2_ref, o2_ref, o3_ref, out_ref,
    inb, xin, p1, p2, p3, wb1, wb2, ue, uo, fbuf, stage, recvb, mixed, uk_ref, vg1, vo1, vg2, vo2, vo3,
    in_send, in_recv, row_send, row_recv, out_send, out_recv, w_sem,
):
    tm = lax.axis_index("tm")
    tile = lax.axis_index("tile")
    zh, core = tm // 2, tm % 2
    big, zl = tile // 2, tile % 2
    z = zh * 2 + zl
    row = big * 2 + core
    has_up = row > 0
    has_down = row < 31

    def holder(r):
        return (zh * 2 + r % 2, (r // 2) * 2 + zl)

    barrier = pltpu.get_barrier_semaphore()
    for zz in range(4):
        for cc in range(2):
            partner = ((zl == cc) | (core == zz % 2)) & ~((z == zz) & (core == cc))

            @pl.when(partner)
            def _():
                pl.semaphore_signal(
                    barrier, inc=1, device_id=((zz // 2) * 2 + cc, big * 2 + zz % 2), device_id_type=MESH
                )

    outer = jnp.where(core == 1, row + 1, row - 1)
    has_outer = (outer >= 0) & (outer < 32)

    @pl.when(has_outer)
    def _():
        pl.semaphore_signal(barrier, inc=1, device_id=holder(outer), device_id_type=MESH)

    loads = [
        pltpu.make_async_copy(ref, to.at[:, :, pl.ds(64, 576)], w_sem.at[i])
        for i, (ref, to) in enumerate(((w1_ref, wb1), (w2_ref, wb2)))
    ]
    small = [
        pltpu.make_async_copy(ref, to, w_sem.at[2 + i])
        for i, (ref, to) in enumerate(
            ((g1_ref, vg1), (o1_ref, vo1), (g2_ref, vg2), (o2_ref, vo2), (o3_ref, vo3))
        )
    ] + [pltpu.make_async_copy(up_ref, uk_ref, w_sem.at[7])]
    for load in small:
        load.start()

    for buf in (wb1, wb2):
        for base in (0, 640):
            buf[:, :, base : base + 64] = jnp.zeros((3, 3, 64, 192), BF16)
    for buf in (p2, p3):
        for b in (6, 41):
            buf[:, 16 * b : 16 * b + 16] = jnp.zeros((3, 16, 384), BF16)

    @pl.when(~has_up)
    def _():
        for buf in (p1, p2, p3):
            buf[0] = jnp.zeros((16 * PAIRS, 384), BF16)

    @pl.when(~has_down)
    def _():
        for buf in (p1, p2, p3):
            buf[2] = jnp.zeros((16 * PAIRS, 384), BF16)

    pl.semaphore_wait(barrier, jnp.where(zl == core, 5, 6) + has_outer.astype(jnp.int32))

    def windows(chunk):
        lo, hi = INPUT[chunk], INPUT[chunk + 1]
        if chunk == 0:
            return ((lambda zz: zz == 0, 8, hi), (lambda zz: zz != 0, lo, hi))
        if chunk == COUNTS[0] - 1:
            return ((lambda zz: zz == 3, lo, 40), (lambda zz: zz != 3, lo, hi))
        return ((lambda zz: zz >= 0, lo, hi),)

    def reshard(chunk, ahead, lo, hi):
        zz = (z + ahead) % 4
        src = x_ref.at[pl.ds(pl.multiple_of(12 * (lo - 8 + 32 * zz), 16), 12 * (hi - lo))]
        dst = inb.at[tm, pl.ds(12 * lo, 12 * (hi - lo))]
        local = pltpu.make_async_copy(src, dst, in_recv.at[chunk])
        remote = pltpu.make_async_remote_copy(
            src_ref=src, dst_ref=dst, send_sem=in_send.at[ahead], recv_sem=in_recv.at[chunk],
            device_id=((zz // 2) * 2 + zl, big * 2 + zz % 2), device_id_type=MESH,
        )
        return zz, local, remote

    for chunk in range(COUNTS[0]):
        for ahead in (2, 1, 3, 0):
            for fits, lo, hi in windows(chunk):
                zz, local, remote = reshard(chunk, ahead, lo, hi)
                if ahead == 0:
                    pl.when(fits(zz) & (zl == core))(local.start)
                    pl.when(fits(zz) & (zl != core))(remote.start)
                else:
                    pl.when(fits(zz))(remote.start)

    for load in loads:
        load.start()

    def wait_input(chunk):
        for fits, lo, hi in windows(chunk):

            ref = inb.at[:, pl.ds(12 * lo, 12 * (hi - lo))]
            pl.when(fits(z))(pltpu.make_async_copy(ref, ref, in_recv.at[chunk]).wait)

    def wait_input_sent(ahead):
        zz = (z + ahead) % 4
        for edge, pairs in (((zz == 0) | (zz == 3), 36), ((zz == 1) | (zz == 2), 40)):
            ref = x_ref.at[pl.ds(0, 12 * pairs)]
            go = edge if ahead else edge & (zl != core)
            pl.when(go)(pltpu.make_async_copy(ref, ref, in_send.at[ahead]).wait)

    for load in small:
        load.wait()
    src_lane = lax.broadcasted_iota(jnp.int32, (96, 256), 0)
    dst_lane = lax.broadcasted_iota(jnp.int32, (96, 256), 1)
    for u_ref, shift in ((ue, 0), (uo, 64)):
        sel_a = jnp.where(dst_lane == src_lane + shift, 1.0, 0.0).astype(BF16)
        sel_b = jnp.where(dst_lane == src_lane + shift + 96, 1.0, 0.0).astype(BF16)
        parts = []
        for q in range(3):
            a = [jnp.dot(uk_ref[q, s], sel_a, preferred_element_type=F32) for s in range(3)]
            b = [jnp.dot(uk_ref[q, s], sel_b, preferred_element_type=F32) for s in range(3)]
            parts.append((a[0], a[1] + a[2] + b[0] + b[1], b[2]))
        for phase, tap, rows in ((0, 0, (0,)), (0, 1, (1, 2)), (1, 0, (0, 1)), (1, 1, (2,))):
            left, mid, right = [
                functools.reduce(lambda m, n: m + n, [parts[q][i] for q in rows]).astype(BF16) for i in range(3)
            ]
            base = 640 * tap
            blank = jnp.zeros((64, 256), BF16)
            order = (mid, right, blank, left) if shift == 0 else (left, mid, right, blank)
            for block in order:
                u_ref[phase, base : base + block.shape[0]] = block
                base += block.shape[0]

    def inside_mask(first, rows):
        pair = lax.broadcasted_iota(jnp.int32, (rows, 128), 0) // 16 + first + (32 * z - 8)
        return (pair >= 0) & (pair < 128)

    bufs = (p1, p2, p3)

    def chunk_rows(st, chunk, end=None):
        lo, hi = BOUNDS[st][chunk], BOUNDS[st][chunk + 1 if end is None else end]
        return pl.ds(16 * lo, 16 * (hi - lo))

    def row_copies(st, chunk):
        buf, rows = bufs[st], chunk_rows(st, chunk)
        copies = []
        for d, (to, slot, exists) in enumerate(((row + 1, 0, has_down), (row - 1, 2, has_up))):
            copies.append((exists, pltpu.make_async_remote_copy(
                src_ref=buf.at[1, rows], dst_ref=buf.at[slot, rows],
                send_sem=row_send.at[st, d], recv_sem=row_recv.at[st, d, chunk],
                device_id=holder(to), device_id_type=MESH,
            )))
        return copies

    def send_rows(st, chunk):
        for exists, copy in row_copies(st, chunk):
            pl.when(exists)(copy.start)

    def wait_sent(st):
        ref = bufs[st].at[1, chunk_rows(st, 0, -1)]
        for d, exists in enumerate((has_down, has_up)):
            pl.when(exists)(pltpu.make_async_copy(ref, ref, row_send.at[st, d]).wait)

    waited = [[0, 0, 0], [0, 0, 0]]

    def wait_rows(st, end, near):
        seen = waited[near]
        while seen[st] < COUNTS[st] and BOUNDS[st][seen[st]] < end:
            chunk = seen[st]
            d = 1 - core if near else core
            ref = bufs[st].at[2 * d, chunk_rows(st, chunk)]
            wait = pltpu.make_async_copy(ref, ref, row_recv.at[st, d, chunk]).wait
            wait() if near else pl.when(has_outer)(wait)
            seen[st] += 1

    lane8 = lax.broadcasted_iota(jnp.int32, (8, 128), 1)

    def widened(ref):
        v = jnp.concatenate([ref[...], jnp.zeros((1, 256 - ref.shape[1]), F32)], axis=1)
        return jnp.broadcast_to(v, (8, 256))

    def doubled(ref):
        v = widened(ref)
        r = pltpu.roll(v, 64, 1)
        return jnp.concatenate([v[:, :128], jnp.where(lane8 < 64, v[:, 128:], r[:, :128]), r[:, 128:]], axis=1)[0:1]

    gain1, off1, gain2, off2 = [doubled(ref) for ref in (vg1, vo1, vg2, vo2)]
    quarter = jnp.concatenate([widened(vo3), jnp.zeros((8, 128), F32)], axis=1)
    off3 = (quarter + pltpu.roll(quarter, 96, 1) + pltpu.roll(quarter, 192, 1) + pltpu.roll(quarter, 288, 1))[0:1]

    def act1_group(i):
        first = 4 + 4 * i
        start = 48 * i + 48
        groups = [inb[g, pl.ds(start, 48), :].astype(F32) for g in range(4)]
        tiles = [
            jnp.concatenate([g[4 * k : 4 * k + 4] for g in groups], axis=0) for k in range(12)
        ]
        x = [jnp.concatenate(tiles[i3::3], axis=0) for i3 in range(3)]
        acts = pair_norm_silu(*x, gain1, inside_mask(first, 64))
        rows = pl.ds(64 * i + 64, 64)
        for n in range(3):
            xin[rows, 128 * n : 128 * (n + 1)] = x[n].astype(BF16)
            p1[1, rows, 128 * n : 128 * (n + 1)] = acts[n]

    def act1(chunk):
        wait_input(chunk)
        for i in range(INPUT[chunk] // 4 - 1, INPUT[chunk + 1] // 4 - 1):
            act1_group(i)
        send_rows(0, chunk)

    def conv(buf, wb, lo, hi):
        m = 16 * (hi - lo)
        here, before, after = (pl.ds(16 * (lo + k), m) for k in (0, -1, 1))
        even, odd = [], []
        for q in range(3):
            even += [buf[q, before, 128:384], buf[q, here, :]]
            odd += [buf[q, here, :], buf[q, after, 0:256]]
        outs = []
        t = lax.broadcasted_iota(jnp.int32, (m, 192), 0) % 16
        for lhs, base in ((even, 0), (odd, 64)):
            lhs = jnp.concatenate(lhs, axis=1)
            y = [
                jnp.dot(lhs, wb[p, :, base : base + 640].reshape(1920, 192), preferred_element_type=F32)
                for p in range(3)
            ]
            total = y[2] + jnp.where(t >= 1, pltpu.roll(y[1], 1, 0), 0.0)
            total = total + jnp.where(t >= 2, pltpu.roll(y[0], 2, 0), 0.0)
            outs.append(total)
        e, o = outs
        blank = jnp.zeros((m, 64), F32)
        o = pltpu.roll(jnp.concatenate([o, blank], axis=1), 64, 1)
        e = jnp.concatenate([e, blank], axis=1)
        return [e[:, :128], e[:, 128:] + o[:, :128], o[:, 128:]]

    def conv1(chunk):
        if chunk == 0:
            loads[0].wait()
        lo, hi = CONV1[chunk], CONV1[chunk + 1]
        wait_rows(0, hi + 1, True)
        wait_rows(0, hi + 1, False)
        x = conv(p1, wb1, lo, hi)
        x = [v + off1[:, 128 * n : 128 * (n + 1)] for n, v in enumerate(x)]
        acts = pair_norm_silu(*x, gain2, inside_mask(lo, 16 * (hi - lo)))
        for n in range(3):
            p2[1, 16 * lo : 16 * hi, 128 * n : 128 * (n + 1)] = acts[n]
        send_rows(1, chunk)

    def conv2(chunk):
        if chunk == 0:
            loads[1].wait()
        lo, hi = CONV2[chunk], CONV2[chunk + 1]
        wait_rows(1, hi + 1, True)
        wait_rows(1, hi + 1, False)
        x = conv(p2, wb2, lo, hi)
        inside = inside_mask(lo, 16 * (hi - lo))
        for n in range(3):
            lanes = slice(128 * n, 128 * (n + 1))
            v = xin[16 * lo : 16 * hi, lanes].astype(F32) + (x[n] + off2[:, lanes])
            p3[1, 16 * lo : 16 * hi, lanes] = jnp.where(inside, v, 0.0).astype(BF16)
        send_rows(2, chunk)

    def upsample(chunk, half):
        lo, hi = UPS[chunk], UPS[chunk + 1]
        wait_rows(2, hi + 1, half == 0)
        phase = core if half else 1 - core
        m = 16 * (hi - lo)
        here, before, after = (pl.ds(16 * (lo + k), m) for k in (0, -1, 1))
        even, odd = [], []
        for q in (phase, phase + 1):
            even += [p3[q, here, :], p3[q, before, 128:384]]
            odd += [p3[q, here, :], p3[q, after, 0:256]]
        e = jnp.dot(jnp.concatenate(even, axis=1), ue[phase], preferred_element_type=F32)
        o = jnp.dot(jnp.concatenate(odd, axis=1), uo[phase], preferred_element_type=F32)
        tiles = [e[:, :128], e[:, 128:] + o[:, :128], o[:, 128:]]
        for i3 in range(3):
            v = tiles[i3] + off3[:, 128 * i3 : 128 * (i3 + 1)]
            for j in range(lo, hi):
                at = 16 * (3 * (j - 8) + i3)
                fbuf[half, at : at + 16, :] = v[16 * (j - lo) : 16 * (j - lo) + 16]
        first, last = OUT_ROWS[chunk], OUT_ROWS[chunk + 1]
        for t in range(16):
            v = fbuf[half, pl.ds(16 * first + t, last - first, stride=16), :]
            stage[half, t, first:last, :] = v.astype(BF16)
        for g in range(4):
            src = stage.at[half, pl.ds(4 * g, 4), pl.ds(first, last - first)]
            dst = recvb.at[half, z, :, pl.ds(first, last - first)]
            mine = (tm == g) & (zl == core)
            pl.when(mine)(pltpu.make_async_copy(src, dst, out_recv.at[half, chunk]).start)
            pl.when(~mine)(pltpu.make_async_remote_copy(
                src_ref=src, dst_ref=dst, send_sem=out_send.at[half, g], recv_sem=out_recv.at[half, chunk],
                device_id=(g, big * 2 + core), device_id_type=MESH,
            ).start)

    def interleave(chunk):
        first, last = OUT_ROWS[chunk], OUT_ROWS[chunk + 1]
        n = last - first
        for half in range(2):
            ref = recvb.at[half, :, :, pl.ds(first, n)]
            pltpu.make_async_copy(ref, ref, out_recv.at[half, chunk]).wait()
        for zz in range(4):
            for f in range(4):
                at = 192 * (4 * zz + f)
                for a in range(2):
                    half = zl if a else 1 - zl
                    mixed[pl.ds(at + a, n, stride=2), :] = recvb[half, zz, f, first:last, :].astype(F32)
                out_ref[f, 192 * zz + 2 * first : 192 * zz + 2 * last, :] = mixed[at : at + 2 * n, :].astype(BF16)

    work = (act1, conv1, conv2, lambda c: upsample(c, 0), lambda c: upsample(c, 1), interleave)
    for stage_chunk in ORDER.split():
        work[int(stage_chunk[0])](int(stage_chunk[1]))

    for ahead in range(4):
        wait_input_sent(ahead)
    for st in range(3):
        wait_sent(st)
    for half in range(2):
        for g in range(4):
            ref = stage.at[half, pl.ds(4 * g, 4)]
            mine = (tm == g) & (zl == core)
            pl.when(~mine)(pltpu.make_async_copy(ref, ref, out_send.at[half, g]).wait)


def shards(features, gain1, kernel1, offset1, gain2, kernel2, offset2, up_kernel, up_offset):
    x = features.reshape(4, 384, 128).transpose(1, 0, 2).reshape(1536, 128)
    small = [v.reshape(1, -1) for v in (gain1, offset1, gain2, offset2, up_offset)]
    dma = pltpu.SemaphoreType.DMA
    act = pltpu.VMEM((3, 16 * PAIRS, 384), BF16)
    weights = pltpu.VMEM((3, 3, 704, 192), BF16)
    out = pl.pallas_call(
        kernel,
        out_shape=pltpu.VMEM((4, 768, 128), BF16),
        in_specs=[pl.BlockSpec(memory_space=pl.ANY)] * 9,
        out_specs=pl.BlockSpec(memory_space=pltpu.VMEM),
        scratch_shapes=[
            pltpu.VMEM((4, 12 * PAIRS, 128), BF16),
            pltpu.VMEM((16 * PAIRS, 384), BF16),
            act, act, act,
            weights, weights,
            pltpu.VMEM((2, 1280, 256), BF16),
            pltpu.VMEM((2, 1280, 256), BF16),
            pltpu.VMEM((2, 16 * 96, 128), F32),
            pltpu.VMEM((2, 16, 96, 128), BF16),
            pltpu.VMEM((2, 4, 4, 96, 128), BF16),
            pltpu.VMEM((16 * 192, 128), F32),
            pltpu.VMEM((3, 3, 192, 96), BF16),
            *[pltpu.VMEM((1, n), F32) for n in (192, 192, 192, 192, 96)],
            dma((4,)), dma((COUNTS[0],)),
            dma((3, 2)), dma((3, 2, MOST)),
            dma((2, 4)), dma((2, COUNTS[3])),
            dma((8,)),
        ],
        compiler_params=pltpu.CompilerParams(
            collective_id=0, has_side_effects=True, vmem_limit_bytes=56 * 1024 * 1024
        ),
    )(x, kernel1.reshape(3, 3, 576, 192), kernel2.reshape(3, 3, 576, 192), up_kernel, *small)
    return out.reshape(4, 384, 2, 128).transpose(0, 2, 1, 3).reshape(4, 2, 49152)


def solution(mesh):
    placed = (P("tm", "tile", None), P(), P(), P(), P(), P(), P(), P(), P())
    return jax.shard_map(
        shards, mesh=mesh, in_specs=placed, out_specs=P("tm", "tile", None), check_vma=False
    )
```

```python
import functools

import jax
import jax.numpy as jnp
from jax import lax
from jax.experimental import pallas as pl
from jax.experimental.pallas import tpu as pltpu
from jax.sharding import PartitionSpec as P

MESH = pl.DeviceIdType.MESH
EPS = 1e-06
F32 = jnp.float32
BF16 = jnp.bfloat16
PAIRS = 48
INPUT = (4, 12, 20, 28, 36, 44)
ACT1 = (6, *INPUT[1:-1], 42)
CONV1 = (7, 18, 26, 34, 41)
CONV2 = (7, 17, 25, 33, 41)
UPS = (8, 16, 24, 32, 40)
BOUNDS = (ACT1, CONV1, CONV2, UPS)
COUNTS = tuple(len(b) - 1 for b in BOUNDS)
MOST = max(COUNTS)
OUT_ROWS = tuple(16 * (3 * (b - 8) // 16) for b in UPS)
ORDER = (
    "00 01 02 10 03 11 04 12 20 21 13 22 30 23 31 40 32 41 50 42 51 33 52 43 60 61 62 53 63 70 71 72 73"
)


def pair_norm_silu(x0, x1, x2, gain, inside):
    low = lax.broadcasted_iota(jnp.int32, x1.shape, 1) < 64
    s1 = x1 * x1
    even = jnp.sum(x0 * x0 + jnp.where(low, s1, 0.0), axis=1, keepdims=True)
    odd = jnp.sum(x2 * x2 + jnp.where(low, 0.0, s1), axis=1, keepdims=True)
    even = lax.rsqrt(even * (1.0 / 192.0) + EPS)
    odd = lax.rsqrt(odd * (1.0 / 192.0) + EPS)
    scales = (even, jnp.where(low, even, odd), odd)
    outs = []
    for i, (x, s) in enumerate(zip((x0, x1, x2), scales)):
        v = x * s * gain[:, 128 * i : 128 * (i + 1)]
        v = 0.5 * v * (1.0 + jnp.tanh(0.5 * v))
        outs.append(inside(v).astype(BF16))
    return outs


def kernel(
    x_ref, w1_ref, w2_ref, up_ref, g1_ref, o1_ref, g2_ref, o2_ref, o3_ref, out_ref,
    inb, xin, p1, p2, p3, wb1, wb2, ue, uo, acc, fbuf, stage, recvb, mixed, uk_ref, vg1, vo1, vg2, vo2, vo3,
    in_send, in_recv, row_send, row_recv, out_send, out_recv, w_sem,
):
    tm = lax.axis_index("tm")
    tile = lax.axis_index("tile")
    zh, core = tm // 2, tm % 2
    big, zl = tile // 2, tile % 2
    z = zh * 2 + zl
    row = big * 2 + core
    has_up = row > 0
    has_down = row < 31

    def holder(r):
        return (zh * 2 + r % 2, (r // 2) * 2 + zl)

    barrier = pltpu.get_barrier_semaphore()
    for zz in range(4):
        for cc in range(2):
            partner = ((zl == cc) | (core == zz % 2)) & ~((z == zz) & (core == cc))

            @pl.when(partner)
            def _():
                pl.semaphore_signal(
                    barrier, inc=1, device_id=((zz // 2) * 2 + cc, big * 2 + zz % 2), device_id_type=MESH
                )

    outer = jnp.where(core == 1, row + 1, row - 1)
    has_outer = (outer >= 0) & (outer < 32)

    @pl.when(has_outer)
    def _():
        pl.semaphore_signal(barrier, inc=1, device_id=holder(outer), device_id_type=MESH)

    loads = [
        pltpu.make_async_copy(ref, to.at[:, :, pl.ds(64, 576)], w_sem.at[i])
        for i, (ref, to) in enumerate(((w1_ref, wb1), (w2_ref, wb2)))
    ]
    small = [
        pltpu.make_async_copy(ref, to, w_sem.at[2 + i])
        for i, (ref, to) in enumerate(
            ((g1_ref, vg1), (o1_ref, vo1), (g2_ref, vg2), (o2_ref, vo2), (o3_ref, vo3))
        )
    ] + [pltpu.make_async_copy(up_ref, uk_ref, w_sem.at[7])]
    for load in small:
        load.start()

    for buf in (wb1, wb2):
        for base in (0, 640):
            buf[:, :, base : base + 64] = jnp.zeros((3, 3, 64, 192), BF16)
    for buf in (p2, p3):
        for b in (6, 41):
            buf[:, 16 * b : 16 * b + 16] = jnp.zeros((3, 16, 384), BF16)

    @pl.when(~has_up)
    def _():
        for buf in (p1, p2, p3):
            buf[0] = jnp.zeros((16 * PAIRS, 384), BF16)

    @pl.when(~has_down)
    def _():
        for buf in (p1, p2, p3):
            buf[2] = jnp.zeros((16 * PAIRS, 384), BF16)

    pl.semaphore_wait(barrier, jnp.where(zl == core, 5, 6) + has_outer.astype(jnp.int32))

    def windows(chunk):
        lo, hi = INPUT[chunk], INPUT[chunk + 1]
        if chunk == 0:
            return ((lambda zz: zz == 0, 8, hi), (lambda zz: zz != 0, lo, hi))
        if chunk == COUNTS[0] - 1:
            return ((lambda zz: zz == 3, lo, 40), (lambda zz: zz != 3, lo, hi))
        return ((lambda zz: zz >= 0, lo, hi),)

    def reshard(chunk, ahead, lo, hi):
        zz = (z + ahead) % 4
        src = x_ref.at[pl.ds(pl.multiple_of(12 * (lo - 8 + 32 * zz), 16), 12 * (hi - lo))]
        dst = inb.at[tm, pl.ds(12 * lo, 12 * (hi - lo))]
        local = pltpu.make_async_copy(src, dst, in_recv.at[chunk])
        remote = pltpu.make_async_remote_copy(
            src_ref=src, dst_ref=dst, send_sem=in_send.at[ahead], recv_sem=in_recv.at[chunk],
            device_id=((zz // 2) * 2 + zl, big * 2 + zz % 2), device_id_type=MESH,
        )
        return zz, local, remote

    for chunk in range(COUNTS[0]):
        for ahead in (2, 1, 3, 0):
            for fits, lo, hi in windows(chunk):
                zz, local, remote = reshard(chunk, ahead, lo, hi)
                if ahead == 0:
                    pl.when(fits(zz) & (zl == core))(local.start)
                    pl.when(fits(zz) & (zl != core))(remote.start)
                else:
                    pl.when(fits(zz))(remote.start)

    for load in loads:
        load.start()

    def wait_input(chunk):
        for fits, lo, hi in windows(chunk):

            ref = inb.at[:, pl.ds(12 * lo, 12 * (hi - lo))]
            pl.when(fits(z))(pltpu.make_async_copy(ref, ref, in_recv.at[chunk]).wait)

    def wait_input_sent(ahead):
        zz = (z + ahead) % 4
        for edge, pairs in (((zz == 0) | (zz == 3), 36), ((zz == 1) | (zz == 2), 40)):
            ref = x_ref.at[pl.ds(0, 12 * pairs)]
            go = edge if ahead else edge & (zl != core)
            pl.when(go)(pltpu.make_async_copy(ref, ref, in_send.at[ahead]).wait)

    for load in small:
        load.wait()
    src_lane = lax.broadcasted_iota(jnp.int32, (96, 256), 0)
    dst_lane = lax.broadcasted_iota(jnp.int32, (96, 256), 1)
    for u_ref, shift in ((ue, 0), (uo, 64)):
        sel_a = jnp.where(dst_lane == src_lane + shift, 1.0, 0.0).astype(BF16)
        sel_b = jnp.where(dst_lane == src_lane + shift + 96, 1.0, 0.0).astype(BF16)
        parts = []
        for q in range(3):
            a = [jnp.dot(uk_ref[q, s], sel_a, preferred_element_type=F32) for s in range(3)]
            b = [jnp.dot(uk_ref[q, s], sel_b, preferred_element_type=F32) for s in range(3)]
            parts.append((a[0], a[1] + a[2] + b[0] + b[1], b[2]))
        for phase, tap, rows in ((0, 0, (0,)), (0, 1, (1, 2)), (1, 0, (0, 1)), (1, 1, (2,))):
            left, mid, right = [
                functools.reduce(lambda m, n: m + n, [parts[q][i] for q in rows]).astype(BF16) for i in range(3)
            ]
            base = 640 * tap
            blank = jnp.zeros((64, 256), BF16)
            order = (mid, right, blank, left) if shift == 0 else (left, mid, right, blank)
            for block in order:
                u_ref[phase, base : base + block.shape[0]] = block
                base += block.shape[0]

    def inside_mask(first, rows):
        if first >= 8 and first + rows // 16 <= 40:
            return lambda v: v
        pair = lax.broadcasted_iota(jnp.int32, (rows, 128), 0) // 16 + first + (32 * z - 8)
        return lambda v: jnp.where((pair >= 0) & (pair < 128), v, 0.0)

    bufs = (p1, p2, p3)

    def chunk_rows(st, chunk, end=None):
        lo, hi = BOUNDS[st][chunk], BOUNDS[st][chunk + 1 if end is None else end]
        return pl.ds(16 * lo, 16 * (hi - lo))

    def row_copies(st, chunk):
        buf, rows = bufs[st], chunk_rows(st, chunk)
        copies = []
        for d, (to, slot, exists) in enumerate(((row + 1, 0, has_down), (row - 1, 2, has_up))):
            copies.append((exists, pltpu.make_async_remote_copy(
                src_ref=buf.at[1, rows], dst_ref=buf.at[slot, rows],
                send_sem=row_send.at[st, d], recv_sem=row_recv.at[st, d, chunk],
                device_id=holder(to), device_id_type=MESH,
            )))
        return copies

    def send_rows(st, chunk):
        for exists, copy in row_copies(st, chunk):
            pl.when(exists)(copy.start)

    def wait_sent(st):
        ref = bufs[st].at[1, chunk_rows(st, 0, -1)]
        for d, exists in enumerate((has_down, has_up)):
            pl.when(exists)(pltpu.make_async_copy(ref, ref, row_send.at[st, d]).wait)

    waited = [[0, 0, 0], [0, 0, 0]]

    def wait_rows(st, end, near):
        seen = waited[near]
        while seen[st] < COUNTS[st] and BOUNDS[st][seen[st]] < end:
            chunk = seen[st]
            d = 1 - core if near else core
            ref = bufs[st].at[2 * d, chunk_rows(st, chunk)]
            wait = pltpu.make_async_copy(ref, ref, row_recv.at[st, d, chunk]).wait
            wait() if near else pl.when(has_outer)(wait)
            seen[st] += 1

    lane8 = lax.broadcasted_iota(jnp.int32, (8, 128), 1)

    def widened(ref):
        v = jnp.concatenate([ref[...], jnp.zeros((1, 256 - ref.shape[1]), F32)], axis=1)
        return jnp.broadcast_to(v, (8, 256))

    def doubled(ref):
        v = widened(ref)
        r = pltpu.roll(v, 64, 1)
        return jnp.concatenate([v[:, :128], jnp.where(lane8 < 64, v[:, 128:], r[:, :128]), r[:, 128:]], axis=1)[0:1]

    gain1, off1, gain2, off2 = [doubled(ref) for ref in (vg1, vo1, vg2, vo2)]
    quarter = jnp.concatenate([widened(vo3), jnp.zeros((8, 128), F32)], axis=1)
    off3 = (quarter + pltpu.roll(quarter, 96, 1) + pltpu.roll(quarter, 192, 1) + pltpu.roll(quarter, 288, 1))[0:1]

    def act1_group(i):
        first = 4 + 4 * i
        start = 48 * i + 48
        groups = [inb[g, pl.ds(start, 48), :].astype(F32) for g in range(4)]
        tiles = [
            jnp.concatenate([g[4 * k : 4 * k + 4] for g in groups], axis=0) for k in range(12)
        ]
        x = [jnp.concatenate(tiles[i3::3], axis=0) for i3 in range(3)]
        acts = pair_norm_silu(*x, gain1, inside_mask(first, 64))
        rows = pl.ds(64 * i + 64, 64)
        for n in range(3):
            xin[rows, 128 * n : 128 * (n + 1)] = x[n].astype(BF16)
            p1[1, rows, 128 * n : 128 * (n + 1)] = acts[n]

    def act1(chunk):
        wait_input(chunk)
        for i in range(INPUT[chunk] // 4 - 1, INPUT[chunk + 1] // 4 - 1):
            act1_group(i)
        send_rows(0, chunk)

    def conv(buf, wb, lo, hi, taps):
        m = 16 * (hi - lo)
        here, before, after = (pl.ds(16 * (lo + k), m) for k in (0, -1, 1))
        even, odd = [], []
        for q in taps:
            even += [buf[q, before, 128:384], buf[q, here, :]]
            odd += [buf[q, here, :], buf[q, after, 0:256]]
        outs = []
        t = lax.broadcasted_iota(jnp.int32, (m, 192), 0) % 16
        for lhs, base in ((even, 0), (odd, 64)):
            lhs = jnp.concatenate(lhs, axis=1)
            y = []
            for p in range(3):
                w = jnp.concatenate([wb[p, q, base : base + 640] for q in taps], axis=0)
                y.append(jnp.dot(lhs, w, preferred_element_type=F32))
            total = y[2] + jnp.where(t >= 1, pltpu.roll(y[1], 1, 0), 0.0)
            total = total + jnp.where(t >= 2, pltpu.roll(y[0], 2, 0), 0.0)
            outs.append(total)
        e, o = outs
        blank = jnp.zeros((m, 64), F32)
        o = pltpu.roll(jnp.concatenate([o, blank], axis=1), 64, 1)
        e = jnp.concatenate([e, blank], axis=1)
        return [e[:, :128], e[:, 128:] + o[:, :128], o[:, 128:]]

    def conv_near(st, chunk):
        if chunk == 0:
            loads[st].wait()
        lo, hi = BOUNDS[st + 1][chunk], BOUNDS[st + 1][chunk + 1]
        wait_rows(st, hi + 1, True)
        x = conv(bufs[st], (wb1, wb2)[st], lo, hi, (1, 2 - 2 * core))
        for n in range(3):
            acc[st, 16 * lo : 16 * hi, 128 * n : 128 * (n + 1)] = x[n]

    def conv_far(st, chunk, whole):
        lo, hi = BOUNDS[st + 1][chunk], BOUNDS[st + 1][chunk + 1]
        if whole:
            if chunk == 0:
                loads[st].wait()
            wait_rows(st, hi + 1, True)
        wait_rows(st, hi + 1, False)
        if whole:
            return conv(bufs[st], (wb1, wb2)[st], lo, hi, (0, 1, 2))
        x = conv(bufs[st], (wb1, wb2)[st], lo, hi, (2 * core,))
        return [v + acc[st, 16 * lo : 16 * hi, 128 * n : 128 * (n + 1)] for n, v in enumerate(x)]

    def conv1(chunk, whole=False):
        lo, hi = CONV1[chunk], CONV1[chunk + 1]
        x = conv_far(0, chunk, whole)
        x = [v + off1[:, 128 * n : 128 * (n + 1)] for n, v in enumerate(x)]
        acts = pair_norm_silu(*x, gain2, inside_mask(lo, 16 * (hi - lo)))
        for n in range(3):
            p2[1, 16 * lo : 16 * hi, 128 * n : 128 * (n + 1)] = acts[n]
        send_rows(1, chunk)

    def conv2(chunk, whole=False):
        lo, hi = CONV2[chunk], CONV2[chunk + 1]
        x = conv_far(1, chunk, whole)
        inside = inside_mask(lo, 16 * (hi - lo))
        for n in range(3):
            lanes = slice(128 * n, 128 * (n + 1))
            v = xin[16 * lo : 16 * hi, lanes].astype(F32) + (x[n] + off2[:, lanes])
            p3[1, 16 * lo : 16 * hi, lanes] = inside(v).astype(BF16)
        send_rows(2, chunk)

    def upsample(chunk, half):
        lo, hi = UPS[chunk], UPS[chunk + 1]
        wait_rows(2, hi + 1, half == 0)
        phase = core if half else 1 - core
        m = 16 * (hi - lo)
        here, before, after = (pl.ds(16 * (lo + k), m) for k in (0, -1, 1))
        even, odd = [], []
        for q in (phase, phase + 1):
            even += [p3[q, here, :], p3[q, before, 128:384]]
            odd += [p3[q, here, :], p3[q, after, 0:256]]
        e = jnp.dot(jnp.concatenate(even, axis=1), ue[phase], preferred_element_type=F32)
        o = jnp.dot(jnp.concatenate(odd, axis=1), uo[phase], preferred_element_type=F32)
        tiles = [e[:, :128], e[:, 128:] + o[:, :128], o[:, 128:]]
        for i3 in range(3):
            v = tiles[i3] + off3[:, 128 * i3 : 128 * (i3 + 1)]
            for j in range(lo, hi):
                at = 16 * (3 * (j - 8) + i3)
                fbuf[half, at : at + 16, :] = v[16 * (j - lo) : 16 * (j - lo) + 16]
        first, last = OUT_ROWS[chunk], OUT_ROWS[chunk + 1]
        for t in range(16):
            v = fbuf[half, pl.ds(16 * first + t, last - first, stride=16), :]
            stage[half, t, first:last, :] = v.astype(BF16)
        for g in range(4):
            src = stage.at[half, pl.ds(4 * g, 4), pl.ds(first, last - first)]
            dst = recvb.at[half, z, :, pl.ds(first, last - first)]
            mine = (tm == g) & (zl == core)
            pl.when(mine)(pltpu.make_async_copy(src, dst, out_recv.at[half, chunk]).start)
            pl.when(~mine)(pltpu.make_async_remote_copy(
                src_ref=src, dst_ref=dst, send_sem=out_send.at[half, g], recv_sem=out_recv.at[half, chunk],
                device_id=(g, big * 2 + core), device_id_type=MESH,
            ).start)

    def interleave(chunk):
        first, last = OUT_ROWS[chunk], OUT_ROWS[chunk + 1]
        n = last - first
        for half in range(2):
            ref = recvb.at[half, :, :, pl.ds(first, n)]
            pltpu.make_async_copy(ref, ref, out_recv.at[half, chunk]).wait()
        for zz in range(4):
            for f in range(4):
                at = 192 * (4 * zz + f)
                for a in range(2):
                    half = zl if a else 1 - zl
                    mixed[pl.ds(at + a, n, stride=2), :] = recvb[half, zz, f, first:last, :].astype(F32)
                out_ref[f, 192 * zz + 2 * first : 192 * zz + 2 * last, :] = mixed[at : at + 2 * n, :].astype(BF16)

    work = (
        act1,
        lambda c: conv_near(0, c), conv1,
        lambda c: conv_near(1, c), conv2,
        lambda c: upsample(c, 0), lambda c: upsample(c, 1), interleave,
        lambda c: conv1(c, True), lambda c: conv2(c, True),
    )
    for stage_chunk in ORDER.split():
        work[int(stage_chunk[0])](int(stage_chunk[1]))

    for ahead in range(4):
        wait_input_sent(ahead)
    for st in range(3):
        wait_sent(st)
    for half in range(2):
        for g in range(4):
            ref = stage.at[half, pl.ds(4 * g, 4)]
            mine = (tm == g) & (zl == core)
            pl.when(~mine)(pltpu.make_async_copy(ref, ref, out_send.at[half, g]).wait)


def shards(features, gain1, kernel1, offset1, gain2, kernel2, offset2, up_kernel, up_offset):
    x = features.reshape(4, 384, 128).transpose(1, 0, 2).reshape(1536, 128)
    small = [v.reshape(1, -1) for v in (gain1, offset1, gain2, offset2, up_offset)]
    dma = pltpu.SemaphoreType.DMA
    act = pltpu.VMEM((3, 16 * PAIRS, 384), BF16)
    weights = pltpu.VMEM((3, 3, 704, 192), BF16)
    out = pl.pallas_call(
        kernel,
        out_shape=pltpu.VMEM((4, 768, 128), BF16),
        in_specs=[pl.BlockSpec(memory_space=pl.ANY)] * 9,
        out_specs=pl.BlockSpec(memory_space=pltpu.VMEM),
        scratch_shapes=[
            pltpu.VMEM((4, 12 * PAIRS, 128), BF16),
            pltpu.VMEM((16 * PAIRS, 384), BF16),
            act, act, act,
            weights, weights,
            pltpu.VMEM((2, 1280, 256), BF16),
            pltpu.VMEM((2, 1280, 256), BF16),
            pltpu.VMEM((2, 16 * PAIRS, 384), F32),
            pltpu.VMEM((2, 16 * 96, 128), F32),
            pltpu.VMEM((2, 16, 96, 128), BF16),
            pltpu.VMEM((2, 4, 4, 96, 128), BF16),
            pltpu.VMEM((16 * 192, 128), F32),
            pltpu.VMEM((3, 3, 192, 96), BF16),
            *[pltpu.VMEM((1, n), F32) for n in (192, 192, 192, 192, 96)],
            dma((4,)), dma((COUNTS[0],)),
            dma((3, 2)), dma((3, 2, MOST)),
            dma((2, 4)), dma((2, COUNTS[3])),
            dma((8,)),
        ],
        compiler_params=pltpu.CompilerParams(
            collective_id=0, has_side_effects=True, vmem_limit_bytes=56 * 1024 * 1024
        ),
    )(x, kernel1.reshape(3, 3, 576, 192), kernel2.reshape(3, 3, 576, 192), up_kernel, *small)
    return out.reshape(4, 384, 2, 128).transpose(0, 2, 1, 3).reshape(4, 2, 49152)


def solution(mesh):
    placed = (P("tm", "tile", None), P(), P(), P(), P(), P(), P(), P(), P())
    return jax.shard_map(
        shards, mesh=mesh, in_specs=placed, out_specs=P("tm", "tile", None), check_vma=False
    )
```

```python
import functools

import jax
import jax.numpy as jnp
from jax import lax
from jax.experimental import pallas as pl
from jax.experimental.pallas import tpu as pltpu
from jax.sharding import PartitionSpec as P

MESH = pl.DeviceIdType.MESH
EPS = 1e-06
F32 = jnp.float32
BF16 = jnp.bfloat16
PAIRS = 48
INPUT = (4, 12, 20, 28, 36, 44)
ACT1 = (6, *INPUT[1:-1], 42)
CONV1 = (7, 18, 26, 34, 41)
CONV2 = (7, 17, 25, 33, 41)
UPS = (8, 16, 24, 32, 40)
BOUNDS = (ACT1, CONV1, CONV2, UPS)
COUNTS = tuple(len(b) - 1 for b in BOUNDS)
MOST = max(COUNTS)
OUT_ROWS = tuple(16 * (3 * (b - 8) // 16) for b in UPS)
ORDER = (
    "00 01 02 10 03 11 04 12 20 21 13 22 30 23 31 40 32 41 50 42 51 33 52 43 60 61 62 53 63 70 71 72 73"
)


def pair_norm_silu(x0, x1, x2, gain, inside):
    low = lax.broadcasted_iota(jnp.int32, x1.shape, 1) < 64
    s1 = x1 * x1
    even = jnp.sum(x0 * x0 + jnp.where(low, s1, 0.0), axis=1, keepdims=True)
    odd = jnp.sum(x2 * x2 + jnp.where(low, 0.0, s1), axis=1, keepdims=True)
    even = lax.rsqrt(even * (1.0 / 192.0) + EPS)
    odd = lax.rsqrt(odd * (1.0 / 192.0) + EPS)
    scales = (even, jnp.where(low, even, odd), odd)
    outs = []
    for i, (x, s) in enumerate(zip((x0, x1, x2), scales)):
        v = x * s * gain[:, 128 * i : 128 * (i + 1)]
        v = 0.5 * v * (1.0 + jnp.tanh(0.5 * v))
        outs.append(inside(v).astype(BF16))
    return outs


def kernel(
    x_ref, w1_ref, w2_ref, up_ref, g1_ref, o1_ref, g2_ref, o2_ref, o3_ref, out_ref,
    inb, xin, p1, p2, p3, wb1, wb2, ue, uo, acc, fbuf, stage, recvb, mixed, uk_ref, vg1, vo1, vg2, vo2, vo3,
    in_send, in_recv, row_send, row_recv, out_send, out_recv, w_sem,
):
    tm = lax.axis_index("tm")
    tile = lax.axis_index("tile")
    zh, core = tm // 2, tm % 2
    big, zl = tile // 2, tile % 2
    z = zh * 2 + zl
    row = big * 2 + core
    has_up = row > 0
    has_down = row < 31

    def holder(r):
        return (zh * 2 + r % 2, (r // 2) * 2 + zl)

    barrier = pltpu.get_barrier_semaphore()
    for zz in range(4):
        for cc in range(2):
            partner = ((zl == cc) | (core == zz % 2)) & ~((z == zz) & (core == cc))

            @pl.when(partner)
            def _():
                pl.semaphore_signal(
                    barrier, inc=1, device_id=((zz // 2) * 2 + cc, big * 2 + zz % 2), device_id_type=MESH
                )

    outer = jnp.where(core == 1, row + 1, row - 1)
    has_outer = (outer >= 0) & (outer < 32)

    @pl.when(has_outer)
    def _():
        pl.semaphore_signal(barrier, inc=1, device_id=holder(outer), device_id_type=MESH)

    loads = [
        pltpu.make_async_copy(ref, to.at[:, :, pl.ds(64, 576)], w_sem.at[i])
        for i, (ref, to) in enumerate(((w1_ref, wb1), (w2_ref, wb2)))
    ]
    small = [
        pltpu.make_async_copy(ref, to, w_sem.at[2 + i])
        for i, (ref, to) in enumerate(
            ((g1_ref, vg1), (o1_ref, vo1), (g2_ref, vg2), (o2_ref, vo2), (o3_ref, vo3))
        )
    ] + [pltpu.make_async_copy(up_ref, uk_ref, w_sem.at[7])]
    for load in small:
        load.start()

    for buf in (wb1, wb2):
        for base in (0, 640):
            buf[:, :, base : base + 64] = jnp.zeros((3, 3, 64, 192), BF16)
    for buf in (p2, p3):
        for b in (6, 41):
            buf[:, 16 * b : 16 * b + 16] = jnp.zeros((3, 16, 384), BF16)

    @pl.when(~has_up)
    def _():
        for buf in (p1, p2, p3):
            buf[0] = jnp.zeros((16 * PAIRS, 384), BF16)

    @pl.when(~has_down)
    def _():
        for buf in (p1, p2, p3):
            buf[2] = jnp.zeros((16 * PAIRS, 384), BF16)

    pl.semaphore_wait(barrier, jnp.where(zl == core, 5, 6) + has_outer.astype(jnp.int32))

    def windows(chunk):
        lo, hi = INPUT[chunk], INPUT[chunk + 1]
        if chunk == 0:
            return ((lambda zz: zz == 0, 8, hi), (lambda zz: zz != 0, lo, hi))
        if chunk == COUNTS[0] - 1:
            return ((lambda zz: zz == 3, lo, 40), (lambda zz: zz != 3, lo, hi))
        return ((lambda zz: zz >= 0, lo, hi),)

    def reshard(chunk, ahead, lo, hi):
        zz = (z + ahead) % 4
        src = x_ref.at[pl.ds(pl.multiple_of(12 * (lo - 8 + 32 * zz), 16), 12 * (hi - lo))]
        dst = inb.at[tm, pl.ds(12 * lo, 12 * (hi - lo))]
        local = pltpu.make_async_copy(src, dst, in_recv.at[chunk])
        remote = pltpu.make_async_remote_copy(
            src_ref=src, dst_ref=dst, send_sem=in_send.at[ahead], recv_sem=in_recv.at[chunk],
            device_id=((zz // 2) * 2 + zl, big * 2 + zz % 2), device_id_type=MESH,
        )
        return zz, local, remote

    for chunk in range(COUNTS[0]):
        for ahead in (1, 3, 2, 0):
            for fits, lo, hi in windows(chunk):
                zz, local, remote = reshard(chunk, ahead, lo, hi)
                if ahead == 0:
                    pl.when(fits(zz) & (zl == core))(local.start)
                    pl.when(fits(zz) & (zl != core))(remote.start)
                else:
                    pl.when(fits(zz))(remote.start)

    for load in loads:
        load.start()

    def wait_input(chunk):
        for fits, lo, hi in windows(chunk):

            ref = inb.at[:, pl.ds(12 * lo, 12 * (hi - lo))]
            pl.when(fits(z))(pltpu.make_async_copy(ref, ref, in_recv.at[chunk]).wait)

    def wait_input_sent(ahead):
        zz = (z + ahead) % 4
        for edge, pairs in (((zz == 0) | (zz == 3), 36), ((zz == 1) | (zz == 2), 40)):
            ref = x_ref.at[pl.ds(0, 12 * pairs)]
            go = edge if ahead else edge & (zl != core)
            pl.when(go)(pltpu.make_async_copy(ref, ref, in_send.at[ahead]).wait)

    for load in small:
        load.wait()
    src_lane = lax.broadcasted_iota(jnp.int32, (96, 256), 0)
    dst_lane = lax.broadcasted_iota(jnp.int32, (96, 256), 1)
    for u_ref, shift in ((ue, 0), (uo, 64)):
        sel_a = jnp.where(dst_lane == src_lane + shift, 1.0, 0.0).astype(BF16)
        sel_b = jnp.where(dst_lane == src_lane + shift + 96, 1.0, 0.0).astype(BF16)
        parts = []
        for q in range(3):
            a = [jnp.dot(uk_ref[q, s], sel_a, preferred_element_type=F32) for s in range(3)]
            b = [jnp.dot(uk_ref[q, s], sel_b, preferred_element_type=F32) for s in range(3)]
            parts.append((a[0], a[1] + a[2] + b[0] + b[1], b[2]))
        for phase, tap, rows in ((0, 0, (0,)), (0, 1, (1, 2)), (1, 0, (0, 1)), (1, 1, (2,))):
            left, mid, right = [
                functools.reduce(lambda m, n: m + n, [parts[q][i] for q in rows]).astype(BF16) for i in range(3)
            ]
            base = 640 * tap
            blank = jnp.zeros((64, 256), BF16)
            order = (mid, right, blank, left) if shift == 0 else (left, mid, right, blank)
            for block in order:
                u_ref[phase, base : base + block.shape[0]] = block
                base += block.shape[0]

    def inside_mask(first, rows):
        if first >= 8 and first + rows // 16 <= 40:
            return lambda v: v
        pair = lax.broadcasted_iota(jnp.int32, (rows, 128), 0) // 16 + first + (32 * z - 8)
        return lambda v: jnp.where((pair >= 0) & (pair < 128), v, 0.0)

    bufs = (p1, p2, p3)

    def chunk_rows(st, chunk, end=None):
        lo, hi = BOUNDS[st][chunk], BOUNDS[st][chunk + 1 if end is None else end]
        return pl.ds(16 * lo, 16 * (hi - lo))

    def row_copies(st, chunk):
        buf, rows = bufs[st], chunk_rows(st, chunk)
        copies = []
        for d, (to, slot, exists) in enumerate(((row + 1, 0, has_down), (row - 1, 2, has_up))):
            copies.append((exists, pltpu.make_async_remote_copy(
                src_ref=buf.at[1, rows], dst_ref=buf.at[slot, rows],
                send_sem=row_send.at[st, d], recv_sem=row_recv.at[st, d, chunk],
                device_id=holder(to), device_id_type=MESH,
            )))
        return copies

    def send_rows(st, chunk):
        for exists, copy in row_copies(st, chunk):
            pl.when(exists)(copy.start)

    def wait_sent(st):
        ref = bufs[st].at[1, chunk_rows(st, 0, -1)]
        for d, exists in enumerate((has_down, has_up)):
            pl.when(exists)(pltpu.make_async_copy(ref, ref, row_send.at[st, d]).wait)

    waited = [[0, 0, 0], [0, 0, 0]]

    def wait_rows(st, end, near):
        seen = waited[near]
        while seen[st] < COUNTS[st] and BOUNDS[st][seen[st]] < end:
            chunk = seen[st]
            d = 1 - core if near else core
            ref = bufs[st].at[2 * d, chunk_rows(st, chunk)]
            wait = pltpu.make_async_copy(ref, ref, row_recv.at[st, d, chunk]).wait
            wait() if near else pl.when(has_outer)(wait)
            seen[st] += 1

    lane8 = lax.broadcasted_iota(jnp.int32, (8, 128), 1)

    def widened(ref):
        v = jnp.concatenate([ref[...], jnp.zeros((1, 256 - ref.shape[1]), F32)], axis=1)
        return jnp.broadcast_to(v, (8, 256))

    def doubled(ref):
        v = widened(ref)
        r = pltpu.roll(v, 64, 1)
        return jnp.concatenate([v[:, :128], jnp.where(lane8 < 64, v[:, 128:], r[:, :128]), r[:, 128:]], axis=1)[0:1]

    gain1, off1, gain2, off2 = [doubled(ref) for ref in (vg1, vo1, vg2, vo2)]
    quarter = jnp.concatenate([widened(vo3), jnp.zeros((8, 128), F32)], axis=1)
    off3 = (quarter + pltpu.roll(quarter, 96, 1) + pltpu.roll(quarter, 192, 1) + pltpu.roll(quarter, 288, 1))[0:1]

    def act1_group(i):
        first = 4 + 4 * i
        start = 48 * i + 48
        groups = [inb[g, pl.ds(start, 48), :].astype(F32) for g in range(4)]
        tiles = [
            jnp.concatenate([g[4 * k : 4 * k + 4] for g in groups], axis=0) for k in range(12)
        ]
        x = [jnp.concatenate(tiles[i3::3], axis=0) for i3 in range(3)]
        acts = pair_norm_silu(*x, gain1, inside_mask(first, 64))
        rows = pl.ds(64 * i + 64, 64)
        for n in range(3):
            xin[rows, 128 * n : 128 * (n + 1)] = x[n].astype(BF16)
            p1[1, rows, 128 * n : 128 * (n + 1)] = acts[n]

    def act1(chunk):
        wait_input(chunk)
        for i in range(INPUT[chunk] // 4 - 1, INPUT[chunk + 1] // 4 - 1):
            act1_group(i)
        send_rows(0, chunk)

    def conv(buf, wb, lo, hi, taps):
        m = 16 * (hi - lo)
        here, before, after = (pl.ds(16 * (lo + k), m) for k in (0, -1, 1))
        even, odd = [], []
        for q in taps:
            even += [buf[q, before, 128:384], buf[q, here, :]]
            odd += [buf[q, here, :], buf[q, after, 0:256]]
        outs = []
        t = lax.broadcasted_iota(jnp.int32, (m, 192), 0) % 16
        for lhs, base in ((even, 0), (odd, 64)):
            lhs = jnp.concatenate(lhs, axis=1)
            y = []
            for p in range(3):
                w = jnp.concatenate([wb[p, q, base : base + 640] for q in taps], axis=0)
                y.append(jnp.dot(lhs, w, preferred_element_type=F32))
            total = y[2] + jnp.where(t >= 1, pltpu.roll(y[1], 1, 0), 0.0)
            total = total + jnp.where(t >= 2, pltpu.roll(y[0], 2, 0), 0.0)
            outs.append(total)
        e, o = outs
        blank = jnp.zeros((m, 64), F32)
        o = pltpu.roll(jnp.concatenate([o, blank], axis=1), 64, 1)
        e = jnp.concatenate([e, blank], axis=1)
        return [e[:, :128], e[:, 128:] + o[:, :128], o[:, 128:]]

    def conv_near(st, chunk):
        if chunk == 0:
            loads[st].wait()
        lo, hi = BOUNDS[st + 1][chunk], BOUNDS[st + 1][chunk + 1]
        wait_rows(st, hi + 1, True)
        x = conv(bufs[st], (wb1, wb2)[st], lo, hi, (1, 2 - 2 * core))
        for n in range(3):
            acc[st, 16 * lo : 16 * hi, 128 * n : 128 * (n + 1)] = x[n]

    def conv_far(st, chunk, whole):
        lo, hi = BOUNDS[st + 1][chunk], BOUNDS[st + 1][chunk + 1]
        if whole:
            if chunk == 0:
                loads[st].wait()
            wait_rows(st, hi + 1, True)
        wait_rows(st, hi + 1, False)
        if whole:
            return conv(bufs[st], (wb1, wb2)[st], lo, hi, (0, 1, 2))
        x = conv(bufs[st], (wb1, wb2)[st], lo, hi, (2 * core,))
        return [v + acc[st, 16 * lo : 16 * hi, 128 * n : 128 * (n + 1)] for n, v in enumerate(x)]

    def conv1(chunk, whole=False):
        lo, hi = CONV1[chunk], CONV1[chunk + 1]
        x = conv_far(0, chunk, whole)
        x = [v + off1[:, 128 * n : 128 * (n + 1)] for n, v in enumerate(x)]
        acts = pair_norm_silu(*x, gain2, inside_mask(lo, 16 * (hi - lo)))
        for n in range(3):
            p2[1, 16 * lo : 16 * hi, 128 * n : 128 * (n + 1)] = acts[n]
        send_rows(1, chunk)

    def conv2(chunk, whole=False):
        lo, hi = CONV2[chunk], CONV2[chunk + 1]
        x = conv_far(1, chunk, whole)
        inside = inside_mask(lo, 16 * (hi - lo))
        for n in range(3):
            lanes = slice(128 * n, 128 * (n + 1))
            v = xin[16 * lo : 16 * hi, lanes].astype(F32) + (x[n] + off2[:, lanes])
            p3[1, 16 * lo : 16 * hi, lanes] = inside(v).astype(BF16)
        send_rows(2, chunk)

    def upsample(chunk, half):
        lo, hi = UPS[chunk], UPS[chunk + 1]
        wait_rows(2, hi + 1, half == 0)
        phase = core if half else 1 - core
        m = 16 * (hi - lo)
        here, before, after = (pl.ds(16 * (lo + k), m) for k in (0, -1, 1))
        even, odd = [], []
        for q in (phase, phase + 1):
            even += [p3[q, here, :], p3[q, before, 128:384]]
            odd += [p3[q, here, :], p3[q, after, 0:256]]
        e = jnp.dot(jnp.concatenate(even, axis=1), ue[phase], preferred_element_type=F32)
        o = jnp.dot(jnp.concatenate(odd, axis=1), uo[phase], preferred_element_type=F32)
        tiles = [e[:, :128], e[:, 128:] + o[:, :128], o[:, 128:]]
        for i3 in range(3):
            v = tiles[i3] + off3[:, 128 * i3 : 128 * (i3 + 1)]
            for j in range(lo, hi):
                at = 16 * (3 * (j - 8) + i3)
                fbuf[half, at : at + 16, :] = v[16 * (j - lo) : 16 * (j - lo) + 16]
        first, last = OUT_ROWS[chunk], OUT_ROWS[chunk + 1]
        for t in range(16):
            v = fbuf[half, pl.ds(16 * first + t, last - first, stride=16), :]
            stage[half, t, first:last, :] = v.astype(BF16)
        for g in range(4):
            src = stage.at[half, pl.ds(4 * g, 4), pl.ds(first, last - first)]
            dst = recvb.at[half, z, :, pl.ds(first, last - first)]
            mine = (tm == g) & (zl == core)
            pl.when(mine)(pltpu.make_async_copy(src, dst, out_recv.at[half, chunk]).start)
            pl.when(~mine)(pltpu.make_async_remote_copy(
                src_ref=src, dst_ref=dst, send_sem=out_send.at[half, g], recv_sem=out_recv.at[half, chunk],
                device_id=(g, big * 2 + core), device_id_type=MESH,
            ).start)

    def interleave(chunk):
        first, last = OUT_ROWS[chunk], OUT_ROWS[chunk + 1]
        n = last - first
        for half in range(2):
            ref = recvb.at[half, :, :, pl.ds(first, n)]
            pltpu.make_async_copy(ref, ref, out_recv.at[half, chunk]).wait()
        for zz in range(4):
            for f in range(4):
                at = 192 * (4 * zz + f)
                for a in range(2):
                    half = zl if a else 1 - zl
                    mixed[pl.ds(at + a, n, stride=2), :] = recvb[half, zz, f, first:last, :].astype(F32)
                out_ref[f, 192 * zz + 2 * first : 192 * zz + 2 * last, :] = mixed[at : at + 2 * n, :].astype(BF16)

    work = (
        act1,
        lambda c: conv_near(0, c), conv1,
        lambda c: conv_near(1, c), conv2,
        lambda c: upsample(c, 0), lambda c: upsample(c, 1), interleave,
        lambda c: conv1(c, True), lambda c: conv2(c, True),
    )
    for stage_chunk in ORDER.split():
        work[int(stage_chunk[0])](int(stage_chunk[1]))

    for ahead in range(4):
        wait_input_sent(ahead)
    for st in range(3):
        wait_sent(st)
    for half in range(2):
        for g in range(4):
            ref = stage.at[half, pl.ds(4 * g, 4)]
            mine = (tm == g) & (zl == core)
            pl.when(~mine)(pltpu.make_async_copy(ref, ref, out_send.at[half, g]).wait)


def shards(features, gain1, kernel1, offset1, gain2, kernel2, offset2, up_kernel, up_offset):
    x = features.reshape(4, 384, 128).transpose(1, 0, 2).reshape(1536, 128)
    small = [v.reshape(1, -1) for v in (gain1, offset1, gain2, offset2, up_offset)]
    dma = pltpu.SemaphoreType.DMA
    act = pltpu.VMEM((3, 16 * PAIRS, 384), BF16)
    weights = pltpu.VMEM((3, 3, 704, 192), BF16)
    out = pl.pallas_call(
        kernel,
        out_shape=pltpu.VMEM((4, 768, 128), BF16),
        in_specs=[pl.BlockSpec(memory_space=pl.ANY)] * 9,
        out_specs=pl.BlockSpec(memory_space=pltpu.VMEM),
        scratch_shapes=[
            pltpu.VMEM((4, 12 * PAIRS, 128), BF16),
            pltpu.VMEM((16 * PAIRS, 384), BF16),
            act, act, act,
            weights, weights,
            pltpu.VMEM((2, 1280, 256), BF16),
            pltpu.VMEM((2, 1280, 256), BF16),
            pltpu.VMEM((2, 16 * PAIRS, 384), F32),
            pltpu.VMEM((2, 16 * 96, 128), F32),
            pltpu.VMEM((2, 16, 96, 128), BF16),
            pltpu.VMEM((2, 4, 4, 96, 128), BF16),
            pltpu.VMEM((16 * 192, 128), F32),
            pltpu.VMEM((3, 3, 192, 96), BF16),
            *[pltpu.VMEM((1, n), F32) for n in (192, 192, 192, 192, 96)],
            dma((4,)), dma((COUNTS[0],)),
            dma((3, 2)), dma((3, 2, MOST)),
            dma((2, 4)), dma((2, COUNTS[3])),
            dma((8,)),
        ],
        compiler_params=pltpu.CompilerParams(
            collective_id=0, has_side_effects=True, vmem_limit_bytes=56 * 1024 * 1024
        ),
    )(x, kernel1.reshape(3, 3, 576, 192), kernel2.reshape(3, 3, 576, 192), up_kernel, *small)
    return out.reshape(4, 384, 2, 128).transpose(0, 2, 1, 3).reshape(4, 2, 49152)


def solution(mesh):
    placed = (P("tm", "tile", None), P(), P(), P(), P(), P(), P(), P(), P())
    return jax.shard_map(
        shards, mesh=mesh, in_specs=placed, out_specs=P("tm", "tile", None), check_vma=False
    )
```
